256 devices in a mesh: dp: 4 (over z_hi, core), expert: 64 (over y, x, z_lo).
Axes of the slice: x: 4, y: 4, z: 8 (z_hi: 2, z_lo: 4; z = z_hi * 4 + z_lo), core: 2. Of those that a mesh axis runs over, the one named last changes fastest.
Arguments:
- tokens: bfloat16 [32768, 2048], P(('dp', 'expert')), may hold values from -6 to 6
- routes: int32 [32768, 8], P(('dp', 'expert')), may hold values from 0 to 63, all different within a row; in each aligned block of 128 rows (0 to 127, 128 to 255, ...) at most 24 rows name the same one
- grad_act: bfloat16 [32768, 8, 768], P(('dp', 'expert')), may hold values from -18 to 18
- owner: int32 [64], replicated, may hold values from 0 to 63, as said below
- moves: int32 [2, 2], replicated, may hold values from 0 to 63, as said below
- weight: bfloat16 [64, 2048, 768], P('expert', 'dp'), may hold values from -5 to 5
- first_moment: bfloat16 [64, 2048, 768], P('expert', 'dp'), may hold values from -4 to 4
- second_moment: bfloat16 [64, 2048, 768], P('expert', 'dp'), may hold values from 0.049804688 to 1
- residual: bfloat16 [4, 64, 2048, 768], P('dp', 'expert'), may hold values from -3 to 3
Outputs:
- new_weight: bfloat16 [64, 2048, 768], P('expert', 'dp')
- new_first_moment: bfloat16 [64, 2048, 768], P('expert', 'dp')
- new_second_moment: bfloat16 [64, 2048, 768], P('expert', 'dp')
The draws below stay inside these ranges and needn't reach their ends.
Inputs may be any that keep to these rules, and one draw needn't show every extreme that they name: `routes`: in each aligned block of 128 rows (the rows of one device) no expert is named by more than 24 rows; in some block some expert is named by exactly 24 rows. `owner`: A permutation: every device of the expert axis owns exactly one expert. `moves`: column 0 lists 2 distinct experts; column 1 gives each its new owner, which is the current owner of another listed expert, so that the listed experts' owners are permuted among themselves and none keeps its own; all other experts keep their owners.
All inputs are finite; a program needn't handle non-finite values.
Results may differ from the reference program's by a relative error of at most 0.018.
Values may be sent and summed in bfloat16 or wider, within the bound.
A program may use at most 128 MiB of HBM per device.

```python
import math
import jax
import jax.numpy as jnp
import numpy as np
from jax import lax

D = 2048
HID = 768
TOP = 8
MOVES = 2
TOK_DEV = 128
EXPERTS = 64
CAP = 24
TOKENS = 32768
N_DP = 4
N_EXPERT = 64


def shared_order(key):
    return jax.random.permutation(key, EXPERTS).astype(jnp.int32)


def draw_owner(key, part):
    return shared_order(key)


def draw_moves(key, part):
    current = shared_order(key)
    key = jax.random.fold_in(key, 5)
    expert_ids = jnp.arange(EXPERTS, dtype=jnp.int32)
    first_pick = jnp.int32(EXPERTS - 1)
    owned_zero = jnp.sum(jnp.where(current == 0, expert_ids, 0)).astype(jnp.int32)
    owned_one = jnp.sum(jnp.where(current == 1, expert_ids, 0)).astype(jnp.int32)
    second_pick = jnp.where(owned_zero == first_pick, owned_one, owned_zero).astype(jnp.int32)
    shuffled = jax.random.permutation(key, EXPERTS).astype(jnp.int32)
    taken = (shuffled == first_pick) | (shuffled == second_pick)
    scores = jnp.arange(EXPERTS, dtype=jnp.int32) + EXPERTS * taken.astype(jnp.int32)
    rest = shuffled[jnp.argsort(scores, stable=True)][:MOVES - 2]
    chosen = jnp.concatenate([jnp.stack([first_pick, second_pick]), rest]).astype(jnp.int32)
    receivers = current[jnp.roll(chosen, 1)]
    return jnp.stack([chosen, receivers], axis=1).astype(jnp.int32)


def block_levels(key, extent, shards, least, top_value):
    gain = 1.0
    for dim, shards_of in shards:
        draws = jax.random.uniform(jax.random.fold_in(jax.random.fold_in(key, 6), dim), (shards_of,), jnp.float32, least / len(shards), top_value / len(shards))
        gain = gain * jnp.repeat(jnp.exp(draws), extent[dim] // shards_of).reshape((-1,) + (1,) * (len(extent) - 1 - dim))
    return gain


def deal_out(stream_key, own, number, rows, count, top, reach, slope):
    ranking = jax.random.permutation(stream_key, count)
    crowded, usual = portions_of(count, rows * top, reach, slope, True), portions_of(count, rows * top, reach, slope, False)
    places = jnp.arange(count)

    def named(lengths, rotation):
        used = int((lengths > 0).sum())
        fixed = max(1, used // 4)
        shifted = fixed + (places - fixed + rotation * (used - fixed)) % max(1, count - fixed)
        return jnp.zeros((count,), jnp.int32).at[ranking[jnp.where(places < fixed, places, shifted)]].set(jnp.asarray(lengths, jnp.int32))

    lengths = jnp.where(number % 4 == 0, named(crowded, number // 4), named(usual, number - number // 4 - 1))
    mixed = jax.random.permutation(jax.random.fold_in(own, 3), count)
    source_of, taker = mixed[0:count // 2 * 2:2], mixed[1:count // 2 * 2:2]
    room = jnp.minimum(lengths[source_of] - 1, reach - lengths[taker]) // 2
    room = jnp.where((source_of == ranking[0]) | (taker == ranking[0]) | (lengths[taker] == 0), 0, jnp.maximum(room, 0))
    shifted = jax.random.randint(jax.random.fold_in(own, 4), (count // 2,), 0, 1 << 20) % (room + 1)
    lengths = lengths.at[source_of].add(-shifted).at[taker].add(shifted)
    items = jnp.searchsorted(jnp.cumsum(lengths), jnp.arange(rows * top), side="right").astype(jnp.int32)
    grid = items.reshape(top, rows).T
    grid = grid[jax.random.permutation(jax.random.fold_in(own, 1), rows)]
    rotation = jax.random.randint(jax.random.fold_in(own, 2), (rows, 1), 0, top)
    return jnp.take_along_axis(grid, (jnp.arange(top)[None, :] + rotation) % top, axis=1)


def portions_of(count, total, limit, lean, full):
    portions = [(1 << 20) // math.isqrt(standing ** lean) + 1 for standing in range(1, count + 1)]
    largest = limit if full else min(limit, max(-(-total // count), total * portions[0] // sum(portions)))
    least = 1 if total - largest >= count - 1 else 0
    counts, surplus = [largest] + [least] * (count - 1), total - largest - least * (count - 1)
    while surplus > 0:
        free = [i for i in range(1, count) if counts[i] < largest] or [i for i in range(1, count) if counts[i] < limit]
        whole, left = sum([portions[i] for i in free]), surplus
        for i in free:
            addition = min(limit - counts[i], max(1, left * portions[i] // whole), surplus)
            counts[i] = counts[i] + addition
            surplus = surplus - addition
    return np.array(counts)


def scatter_about(rng, extent, scale, limit, cuts=(), kind=jnp.bfloat16):
    result = jax.random.normal(rng, extent, jnp.float32) * scale
    if len(cuts) > 0:
        result = block_levels(rng, extent, cuts, -0.22, 0.18) * result
    return jnp.clip(result, min=-limit, max=limit).astype(kind)


def setup_inputs(seed: int = 0) -> dict:
    arg_keys = jax.random.split(jax.random.key(seed), 10)
    tokens = scatter_about(arg_keys[0], (TOKENS, D), 1.0, 6.0, ((0, 256),))
    routes_keys = jax.random.split(jax.random.fold_in(arg_keys[1], 1), TOKENS // TOK_DEV)
    routes_turns = jax.random.permutation(jax.random.fold_in(arg_keys[1], 3), TOKENS // TOK_DEV)
    routes = jax.vmap(lambda own, number: deal_out(jax.random.fold_in(arg_keys[1], 2), own, number, TOK_DEV, EXPERTS, TOP, CAP, 2))(routes_keys, routes_turns).reshape((TOKENS, TOP))
    grad_act = scatter_about(arg_keys[2], (TOKENS, TOP, HID), 3.0, 18.0, ((0, 256),))
    owner = draw_owner(jax.random.fold_in(arg_keys[9], 71), 0)
    moves = draw_moves(jax.random.fold_in(arg_keys[9], 71), 0)
    weight = scatter_about(arg_keys[5], (EXPERTS, D, HID), 0.5, 5.0, ((0, 64), (1, 4)))
    first_moment = scatter_about(arg_keys[6], (EXPERTS, D, HID), 0.5, 4.0, ((0, 64), (1, 4)))
    second_moment = jnp.clip(jnp.exp(math.log(1.0) - 2.9996462 * jax.random.uniform(arg_keys[7], (EXPERTS, D, HID), jnp.float32) ** block_levels(arg_keys[7], (EXPERTS, D, HID), ((0, 64), (1, 4)), -0.2, 0.2)), 0.049804688, 1.0).astype(jnp.bfloat16)
    residual = scatter_about(arg_keys[8], (N_DP, EXPERTS, D, HID), 0.3, 3.0, ((0, 4), (1, 64)))
    return dict(tokens=tokens, routes=routes, grad_act=grad_act, owner=owner, moves=moves, weight=weight, first_moment=first_moment, second_moment=second_moment, residual=residual)


beta_one = 0.9
beta_two = 0.95
step_size = 0.05
epsilon = 1e-08

def silu_slope(values):
    sigma = jax.nn.sigmoid(values)
    return sigma * (1.0 + values * (1.0 - sigma))

def expert_table(flat_routes):
    pair_count = flat_routes.shape[0]
    sorted_ids = jnp.argsort(flat_routes, stable=True).astype(jnp.int32)
    ranked = flat_routes[sorted_ids]
    totals = jnp.zeros((EXPERTS,), jnp.int32).at[flat_routes].add(1)
    starts = jnp.cumsum(totals) - totals
    slot_rank = jnp.arange(pair_count, dtype=jnp.int32) - starts[ranked]
    slot_width = N_EXPERT * CAP
    slot_table = jnp.zeros((EXPERTS, slot_width), jnp.int32).at[ranked, slot_rank].set(sorted_ids)
    slot_valid = jnp.zeros((EXPERTS, slot_width), jnp.int32).at[ranked, slot_rank].set(1)
    return (slot_table, slot_valid)

def reference(tokens, routes, grad_act, owner, moves, weight, first_moment, second_moment, residual):
    new_owner = owner.at[moves[:, 0]].set(moves[:, 1])
    feature_scale = float(D) ** (-0.5)
    group_rows = N_EXPERT * TOK_DEV
    tables = []
    for group_id in range(N_DP):
        group_routes = routes[group_id * group_rows:(group_id + 1) * group_rows].reshape(-1)
        tables.append(expert_table(group_routes))

    def one_expert(expert):
        slot_id = owner[expert]
        w_expert = weight[slot_id]
        grad_total = jnp.zeros((D, HID), jnp.float32)
        for group_id in range(N_DP):
            slot_table, slot_valid = tables[group_id]
            row_picks = slot_table[expert]
            keep_row = slot_valid[expert][:, None] > 0
            x_group = tokens[group_id * group_rows:(group_id + 1) * group_rows]
            g_group = grad_act[group_id * group_rows:(group_id + 1) * group_rows].reshape(-1, HID)
            rows_x = jnp.where(keep_row, x_group[row_picks // TOP], jnp.zeros((), tokens.dtype))
            rows_g = jnp.where(keep_row, g_group[row_picks], jnp.zeros((), grad_act.dtype))
            pre_act = jnp.dot(rows_x, w_expert, preferred_element_type=jnp.float32) * feature_scale
            slope_rows = (rows_g.astype(jnp.float32) * silu_slope(pre_act)).astype(jnp.bfloat16)
            group_term = lax.dot_general(rows_x, slope_rows, (((0,), (0,)), ((), ())), preferred_element_type=jnp.float32) * feature_scale
            group_term = (group_term + residual[group_id, slot_id].astype(jnp.float32)).astype(jnp.bfloat16)
            grad_total = grad_total + group_term.astype(jnp.float32)
        moment_one = beta_one * first_moment[slot_id].astype(jnp.float32) + (1.0 - beta_one) * grad_total
        moment_two = beta_two * second_moment[slot_id].astype(jnp.float32) + (1.0 - beta_two) * grad_total * grad_total
        updated = w_expert.astype(jnp.float32) - step_size * moment_one / (jnp.sqrt(moment_two) + epsilon)
        return (updated.astype(jnp.bfloat16), moment_one.astype(jnp.bfloat16), moment_two.astype(jnp.bfloat16))
    results = lax.map(one_expert, jnp.arange(EXPERTS, dtype=jnp.int32))
    new_weight = jnp.zeros_like(weight).at[new_owner].set(results[0])
    new_first_moment = jnp.zeros_like(first_moment).at[new_owner].set(results[1])
    new_second_moment = jnp.zeros_like(second_moment).at[new_owner].set(results[2])
    return (new_weight, new_first_moment, new_second_moment)
```

```python
import functools

import jax
import jax.numpy as jnp
from jax import lax
from jax.experimental import pallas as pl
from jax.experimental.pallas import tpu as pltpu
from jax.sharding import PartitionSpec as P

MESH = pl.DeviceIdType.MESH
F32 = jnp.float32
BF16 = jnp.bfloat16

beta_one = 0.9
beta_two = 0.95
step_size = 0.05
epsilon = 1e-08

NY, NX, NZ = 4, 4, 4
PLANE = NY * NX
CAP = 24
TOP = 8


def silu_slope(values):
    sigma = jax.nn.sigmoid(values)
    return sigma * (1.0 + values * (1.0 - sigma))


def slot_codes(target, ranks, device_col):
    rank = jnp.sum(jnp.where(device_col == target, ranks, 0.0), axis=0, keepdims=True)
    return target * CAP + rank.astype(jnp.int32)


def targets(routes_row, owner_col, device_col):
    return jnp.sum(jnp.where(device_col == routes_row, owner_col, 0), axis=0, keepdims=True)


class Swap:
    def __init__(self, src, places, spot, at, remote, scratch):
        (self.got1, self.kept1, self.got2, self.kept2, self.got3, self.kept3, self.got4, self.back, self.got,
         self.sent, self.come) = scratch
        self.src, self.places, self.at, self.remote = src, places, at, remote
        self.y, self.x, self.z = spot
        self.half = src.shape[1] // 2
        self.piece = self.half // 4
        self.small = self.piece // 4

    def peer(self, half, first, d):
        if first == (half == 0):
            to = lax.rem(self.x + d, NX)
            return to, self.at(self.y * NX + to, self.z), self.x
        to = lax.rem(self.y + d, NY)
        return to, self.at(to * NX + self.x, self.z), self.y

    def where(self, half, first, slot):
        return self.places[2 + 3 * slot + (1 if first == (half == 0) else 0)]

    def rows1(self, half, to):
        return pl.ds(pl.multiple_of(half * self.half + to * self.piece, 16), self.piece)

    def copy1(self, half, d, arriving=False):
        to, device, mine = self.peer(half, True, d)
        return self.remote(self.src.at[:, self.rows1(half, to)], self.got1.at[half, to if arriving else mine],
                           self.sent.at[0, half, to], self.come.at[0, half, to if arriving else mine], device)

    def copy2(self, half, d, arriving=False):
        to, device, mine = self.peer(half, False, d)
        return self.remote(self.kept1.at[half, :, :, pl.ds(pl.multiple_of(to * self.small, 16), self.small)],
                           self.got2.at[half, to if arriving else mine],
                           self.sent.at[1, half, to], self.come.at[1, half, to if arriving else mine], device)

    def copy3(self, half, d, arriving=False):
        to = lax.rem(self.z + d, NZ)
        device = self.at(self.y * NX + self.x, to)
        return self.remote(self.kept2.at[half], self.got3.at[half, to if arriving else self.z],
                           self.sent.at[2, half, to], self.come.at[2, half, to if arriving else self.z], device)

    def copy4(self, half, d, arriving=False):
        to, device, mine = self.peer(half, False, d)
        return self.remote(self.kept3.at[half], self.got4.at[half, to if arriving else mine],
                           self.sent.at[3, half, to], self.come.at[3, half, to if arriving else mine], device)

    def copy5(self, half, d, arriving=False):
        to, device, mine = self.peer(half, True, d)
        return self.remote(self.back.at[half, to], self.got.at[:, self.rows1(half, to if arriving else mine)],
                           self.sent.at[4, half, to], self.come.at[4, half, to if arriving else mine], device)

    def each(self, act):
        for d in (1, 3, 2):
            for half in range(2):
                act(half, d)

    def start(self):
        self.each(lambda half, d: self.copy1(half, d).start())
        for half in range(2):
            mine = self.peer(half, True, 0)[0]
            self.got1[half, mine] = self.src[:, self.rows1(half, mine), :]

    def second(self):
        self.each(lambda half, d: self.copy1(half, d, True).wait_recv())
        for half in range(2):
            for slot in range(2):
                self.kept1[half, slot] = self.got1[half, self.where(half, True, slot)]
        self.each(lambda half, d: self.copy2(half, d).start())
        for half in range(2):
            mine = self.peer(half, False, 0)[0]
            self.got2[half, mine] = self.kept1[half, :, :, pl.ds(pl.multiple_of(mine * self.small, 16), self.small), :]

    def along_z(self):
        self.each(lambda half, d: self.copy2(half, d, True).wait_recv())
        for half in range(2):
            for slot in range(2):
                self.kept2[half, slot] = self.got2[half, self.where(half, False, slot), slot]
        self.each(lambda half, d: self.copy3(half, d).start())
        for half in range(2):
            self.got3[half, self.z] = self.kept2[half]

    def fourth(self):
        self.each(lambda half, d: self.copy3(half, d, True).wait_recv())
        for half in range(2):
            for slot in range(2):
                self.kept3[half, slot] = self.got3[half, self.places[4 + 3 * slot], slot]
        self.each(lambda half, d: self.copy4(half, d).start())
        for half in range(2):
            self.got4[half, self.peer(half, False, 0)[0]] = self.kept3[half]

    def last(self):
        self.each(lambda half, d: self.copy4(half, d, True).wait_recv())
        for d in (1, 3, 2, 0):
            for half in range(2):
                to, device, _ = self.peer(half, True, d)
                slot = jnp.where(self.places[1] == device[1], 0, 1)
                for i in range(4):
                    rows = pl.ds(i * self.small, self.small)
                    if d:
                        self.back[half, to, :, rows, :] = self.got4[half, i, slot]
                    else:
                        first = pl.multiple_of(half * self.half + to * self.piece + i * self.small, 16)
                        self.got[:, pl.ds(first, self.small), :] = self.got4[half, i, slot]
                if d:
                    self.copy5(half, d).start()

    def wait_last(self):
        self.each(lambda half, d: self.copy5(half, d, True).wait_recv())

    def wait_first(self):
        self.each(lambda half, d: self.copy1(half, d).wait_send())

    def wait_sent(self):
        for copy in (self.copy2, self.copy3, self.copy4, self.copy5):
            self.each(lambda half, d: copy(half, d).wait_send())


def swap_scratch(parts, rows, hidden):
    piece, small = rows // 8, rows // 32
    return [
        pltpu.VMEM((2, 4, parts, piece, hidden), BF16),
        pltpu.VMEM((2, 2, parts, piece, hidden), BF16),
        pltpu.VMEM((2, 4, 2, parts, small, hidden), BF16),
        pltpu.VMEM((2, 2, parts, small, hidden), BF16),
        pltpu.VMEM((2, 4, 2, parts, small, hidden), BF16),
        pltpu.VMEM((2, 2, parts, small, hidden), BF16),
        pltpu.VMEM((2, 4, 2, parts, small, hidden), BF16),
        pltpu.VMEM((2, 4, parts, piece, hidden), BF16),
        pltpu.VMEM((parts, rows, hidden), BF16),
        pltpu.SemaphoreType.DMA((5, 2, 4)),
        pltpu.SemaphoreType.DMA((5, 2, 4)),
    ]


def kernel(
    places, routes_t, routes_f, owner_col, tokens, grads, w_shard, m_shard, v_shard, residual,
    w_out, m_out, v_out,
    codes, all_tokens, packed_x, rows_x, packed_g, relay_g, rows_g, w_full, pre, slopes,
    term, pair_got, z_send, z_got,
    local_sem, tok_up, tok_dn, tok_got, code_up, code_dn, code_got,
    x_sent, x_got, g_sent, g_got, gz_sent, gz_got, w_sent, w_got, t_sent, t_got,
    added, state, grad_small, *swaps,
):
    count = owner_col.shape[0]
    tok_rows, feats = tokens.shape
    hidden = grads.shape[1]
    pairs = grads.shape[0]
    shard_rows = w_shard.shape[0]
    scale = float(feats) ** -0.5

    dp = lax.axis_index("dp")
    me = lax.axis_index("expert")
    z_hi, core = dp // 2, dp % 2
    yx, z = me // NZ, me % NZ
    y, x = yx // NX, yx % NX

    def at(yx_to, z_to):
        return (dp, yx_to * NZ + z_to)

    core_peer = (z_hi * 2 + 1 - core, me)
    far_peer = ((1 - z_hi) * 2 + core, me)

    def plane_peer(dy, dx):
        return lax.rem(y + dy, NY) * NX + lax.rem(x + dx, NX)

    def remote(src, dst, sent, got, to):
        return pltpu.make_async_remote_copy(
            src_ref=src, dst_ref=dst, send_sem=sent, recv_sem=got, device_id=to, device_id_type=MESH
        )

    offsets = [(dy, dx) for dy in range(NY) for dx in range(NX) if dy or dx]

    loads = [
        pltpu.make_async_copy(tokens, all_tokens.at[z], local_sem.at[4]),
        pltpu.make_async_copy(w_shard, state.at[0], local_sem.at[5]),
        pltpu.make_async_copy(m_shard, state.at[1], local_sem.at[6]),
        pltpu.make_async_copy(v_shard, state.at[2], local_sem.at[7]),
        pltpu.make_async_copy(residual, added, local_sem.at[8]),
    ]
    for load in loads:
        load.start()

    barrier = pltpu.get_barrier_semaphore()
    for dy, dx in offsets:
        pl.semaphore_signal(barrier, inc=1, device_id=at(plane_peer(dy, dx), z), device_id_type=MESH)
    for dz in range(1, NZ):
        pl.semaphore_signal(barrier, inc=1, device_id=at(yx, lax.rem(z + dz, NZ)), device_id_type=MESH)
    pl.semaphore_signal(barrier, inc=1, device_id=core_peer, device_id_type=MESH)
    pl.semaphore_signal(barrier, inc=1, device_id=far_peer, device_id_type=MESH)
    pl.semaphore_wait(barrier, len(offsets) + NZ - 1 + 2)

    device_col = lax.broadcasted_iota(jnp.int32, (count, 1), 0)
    own_col = owner_col[...]
    before = (
        lax.broadcasted_iota(jnp.int32, (tok_rows, tok_rows), 0)
        < lax.broadcasted_iota(jnp.int32, (tok_rows, tok_rows), 1)
    ).astype(F32).astype(BF16)
    row_targets = [targets(routes_t[k : k + 1, :], own_col, device_col) for k in range(TOP)]
    member = jnp.zeros((count, tok_rows), F32)
    for k in range(TOP):
        member = member + jnp.where(device_col == row_targets[k], 1.0, 0.0)
    ranks = jnp.dot(member.astype(BF16), before, preferred_element_type=F32)
    codes[z] = jnp.concatenate([slot_codes(t, ranks, device_col) for t in row_targets], axis=0)
    loads[0].wait()

    def hop(source, up):
        step = 1 if up else -1
        to = at(yx, z + step)
        sems = (tok_up, code_up) if up else (tok_dn, code_dn)
        return (
            remote(all_tokens.at[source], all_tokens.at[source], sems[0].at[source], tok_got.at[source], to),
            remote(codes.at[source], codes.at[source], sems[1].at[source], code_got.at[source], to),
        )

    def send_hop(source):
        @pl.when((source <= z) & (z < NZ - 1))
        def _():
            for copy in hop(source, True):
                copy.start()

        @pl.when((source >= z) & (z > 0))
        def _():
            for copy in hop(source, False):
                copy.start()

    def wait_hop(source, up):
        for copy in hop(source, up):
            copy.wait_recv()

    send_hop(z)

    ranked = []
    carry = jnp.zeros((count, 1), F32)
    flat_target = targets(routes_f[...], own_col, device_col)
    for c in range(pairs // tok_rows):
        part = flat_target[:, c * tok_rows : (c + 1) * tok_rows]
        hits = jnp.where(device_col == part, 1.0, 0.0)
        ranked.append(jnp.dot(hits.astype(BF16), before, preferred_element_type=F32) + carry)
        carry = carry + jnp.sum(hits, axis=1, keepdims=True)
    flat_codes = slot_codes(flat_target, jnp.concatenate(ranked, axis=1), device_col)

    group = NX * NZ * CAP

    def g_plane(to):
        return remote(packed_g.at[to], relay_g.at[yx], g_sent.at[to], g_got.at[yx], at(to, z))

    for dy in range(NY):
        y_to = lax.rem(y + dy, NY)
        slot = lax.broadcasted_iota(jnp.int32, (group, pairs), 0) + y_to * group
        pick = jnp.where(slot == flat_codes, 1.0, 0.0).astype(BF16)
        got = jnp.dot(pick, grads[...], preferred_element_type=F32)
        for x_to in range(NX):
            for z_to in range(NZ):
                first = (x_to * NZ + z_to) * CAP
                packed_g[y_to * NX + x_to, z_to] = got[first : first + CAP].astype(BF16)
        for dx in range(NX):
            if dy or dx:
                g_plane(plane_peer(dy, dx)).start()
    self_g = pltpu.make_async_copy(packed_g.at[yx], relay_g.at[yx], local_sem.at[0])
    self_g.start()

    block = 2 * CAP

    def x_plane(pair, to):
        return remote(
            packed_x.at[pair, pl.ds(to * block, block)],
            rows_x.at[pl.ds((pair * PLANE + yx) * block, block)],
            x_sent.at[pair, to], x_got.at[pair, yx], at(to, z),
        )

    def pack_pair(pair, slot):
        part = NX * block
        s = lax.broadcasted_iota(jnp.int32, (part, tok_rows), 0)
        to = (s * 1366) >> 16
        half = (s * 2731) >> 16
        for dy in range(NY):
            y_to = lax.rem(y + dy, NY)
            rank = s - half * CAP
            want = ((y_to * NX + to) * NZ + z) * CAP + rank
            picks = []
            for sub in range(2):
                source = codes[pair * 2 + sub]
                mine = jnp.where(half == 2 * to + sub, want, -1)
                hit = jnp.zeros((part, tok_rows), F32)
                for k in range(TOP):
                    hit = hit + jnp.where(mine == source[k : k + 1, :], 1.0, 0.0)
                picks.append(hit.astype(BF16))
            pick = jnp.concatenate(picks, axis=1)
            both = all_tokens[pl.ds(pair * 2, 2)].reshape(2 * tok_rows, feats)
            rows = pl.ds(pl.multiple_of(y_to * part, 16), part)
            packed_x[pair, rows, :] = jnp.dot(pick, both, preferred_element_type=F32).astype(BF16)
            for dx in range(NX):
                if dy or dx:
                    x_plane(pair, plane_peer(dy, dx)).start()
        pltpu.make_async_copy(
            packed_x.at[pair, pl.ds(yx * block, block)],
            rows_x.at[pl.ds((pair * PLANE + yx) * block, block)],
            local_sem.at[slot],
        ).start()

    def wait_pair(pair, slot):
        for dy, dx in offsets:
            src = plane_peer(dy, dx)
            remote(
                packed_x.at[pair, pl.ds(src * block, block)],
                rows_x.at[pl.ds((pair * PLANE + src) * block, block)],
                x_sent.at[pair, src], x_got.at[pair, src], at(src, z),
            ).wait_recv()
        pltpu.make_async_copy(
            packed_x.at[pair, pl.ds(yx * block, block)],
            rows_x.at[pl.ds((pair * PLANE + yx) * block, block)],
            local_sem.at[slot],
        ).wait()

    def take_hop(distance):
        @pl.when(z >= distance)
        def _():
            wait_hop(z - distance, True)
            send_hop(z - distance)

        @pl.when(z + distance < NZ)
        def _():
            wait_hop(z + distance, False)
            send_hop(z + distance)

    my_pair = z // 2
    take_hop(1)
    pack_pair(my_pair, 1)
    take_hop(2)

    def w_rows(owner_dp):
        return w_full.at[pl.ds(pl.multiple_of(owner_dp * shard_rows, 16), shard_rows)]

    for load in loads[1:4]:
        load.wait()
    w_full[pl.ds(pl.multiple_of(dp * shard_rows, 16), shard_rows), :] = state[0]
    far_dp = (1 - z_hi) * 2 + core
    near_dp = z_hi * 2 + 1 - core
    w_far = remote(state.at[0], w_rows(dp), w_sent.at[0], w_got.at[0], far_peer)
    w_near = remote(state.at[0], w_rows(dp), w_sent.at[1], w_got.at[1], core_peer)
    w_pass = remote(w_rows(far_dp), w_rows(far_dp), w_sent.at[2], w_got.at[2], core_peer)
    w_far.start()
    w_near.start()

    take_hop(3)
    pack_pair(1 - my_pair, 2)

    half_swap = len(swaps) // 2
    swap_state = Swap(state, places, (y, x, z), at, remote, swaps[:half_swap])
    swap_grad = Swap(grad_small, places, (y, x, z), at, remote, swaps[half_swap:])
    swap_state.start()

    for dy, dx in offsets:
        src = plane_peer(dy, dx)
        remote(packed_g.at[src], relay_g.at[src], g_sent.at[src], g_got.at[src], at(src, z)).wait_recv()
    self_g.wait()

    def g_line(z_to, z_from):
        return remote(relay_g.at[:, z_to], rows_g.at[z_from], gz_sent.at[z_to], gz_got.at[z_from], at(yx, z_to))

    for dz in range(1, NZ):
        g_line(lax.rem(z + dz, NZ), z).start()
    self_rows = pltpu.make_async_copy(relay_g.at[:, z], rows_g.at[z], local_sem.at[3])
    self_rows.start()

    w_far.wait_recv()
    w_pass.start()
    w_near.wait_recv()
    w_pass.wait_recv()

    def wait_line(z_from):
        remote(
            relay_g.at[:, z_from], rows_g.at[z_from], gz_sent.at[z_from], gz_got.at[z_from], at(yx, z_from)
        ).wait_recv()

    def forward(pair):
        per = PLANE // 2
        for part in range(2):
            base = pl.multiple_of((pair * PLANE + part * per) * block, 16)
            pre[pl.ds(0, per * block), :] = jnp.dot(
                rows_x[pl.ds(base, per * block), :], w_full[...], preferred_element_type=F32
            ) * scale

            def body(i, _):
                rows = pl.ds(pl.multiple_of(i * block, 16), block)
                src = part * per + i
                g = jnp.concatenate(
                    [rows_g[pair * 2, src].astype(F32), rows_g[pair * 2 + 1, src].astype(F32)], axis=0
                )
                slope = (g * silu_slope(pre[rows, :])).astype(BF16)
                slopes[pl.ds(pl.multiple_of(base + i * block, 16), block), :] = slope
                return 0

            lax.fori_loop(0, per, body, 0)

    wait_pair(my_pair, 1)
    for dz in range(1, NZ):
        wait_line(lax.rem(z + dz, NZ))
    self_rows.wait()
    forward(my_pair)
    wait_pair(1 - my_pair, 2)
    forward(1 - my_pair)
    swap_state.second()

    tile = shard_rows // 2

    def gradient(shard):
        def body(i, _):
            first = pl.multiple_of(shard * shard_rows + i * tile, 128)
            part = lax.dot_general(
                rows_x[:, pl.ds(first, tile)], slopes[...], (((0,), (0,)), ((), ())),
                preferred_element_type=F32,
            )
            total = part * scale + added[pl.ds(first, tile), :].astype(F32)
            term[shard, pl.ds(pl.multiple_of(i * tile, 16), tile), :] = total.astype(BF16)
            return 0

        lax.fori_loop(0, 2, body, 0)

    def to_core(z_hi_of):
        shard = z_hi_of * 2 + 1 - core
        return remote(term.at[shard], pair_got.at[z_hi_of], t_sent.at[z_hi_of], t_got.at[z_hi_of], core_peer)

    loads[4].wait()
    gradient(far_dp + 1 - 2 * core)
    to_core(1 - z_hi).start()
    gradient(far_dp)
    to_core(1 - z_hi).wait_recv()
    z_send[...] = (term[far_dp].astype(F32) + pair_got[1 - z_hi].astype(F32)).astype(BF16)
    z_copy = remote(z_send, z_got, t_sent.at[2], t_got.at[2], far_peer)
    z_copy.start()
    swap_state.along_z()
    gradient(near_dp)
    to_core(z_hi).start()
    gradient(dp)
    swap_state.fourth()
    to_core(z_hi).wait_recv()
    z_copy.wait_recv()
    grad_total = pre
    grad_total[pl.ds(0, shard_rows), :] = term[dp].astype(F32) + pair_got[z_hi].astype(F32) + z_got[...].astype(F32)
    grad_small[0] = grad_total[pl.ds(0, shard_rows), :].astype(BF16)

    swap_grad.start()
    swap_state.last()
    swap_grad.second()
    swap_grad.along_z()
    swap_grad.fourth()
    swap_grad.last()
    swap_state.wait_last()
    swap_grad.wait_last()

    swap_state.wait_first()
    w_far.wait_send()
    w_near.wait_send()
    moved = (places[0] == me) | (places[1] == me)

    def update(i, _):
        rows = pl.ds(pl.multiple_of(i * 64, 16), 64)
        total = jnp.where(moved, swap_grad.got[0, rows, :].astype(F32), grad_total[rows, :])
        old = [
            jnp.where(moved, swap_state.got[c, rows, :].astype(F32), state[c, rows, :].astype(F32))
            for c in range(3)
        ]
        moment_one = beta_one * old[1] + (1.0 - beta_one) * total
        moment_two = beta_two * old[2] + (1.0 - beta_two) * total * total
        state[0, rows, :] = (old[0] - step_size * moment_one / (jnp.sqrt(moment_two) + epsilon)).astype(BF16)
        state[1, rows, :] = moment_one.astype(BF16)
        state[2, rows, :] = moment_two.astype(BF16)
        return 0

    lax.fori_loop(0, shard_rows // 64, update, 0)
    stores = [
        pltpu.make_async_copy(state.at[c], out, local_sem.at[5 + c]) for c, out in enumerate((w_out, m_out, v_out))
    ]
    for store in stores:
        store.start()

    for source in range(NZ):

        @pl.when((source <= z) & (z < NZ - 1))
        def _():
            for copy in hop(source, True):
                copy.wait_send()

        @pl.when((source >= z) & (z > 0))
        def _():
            for copy in hop(source, False):
                copy.wait_send()

    for dy, dx in offsets:
        to = plane_peer(dy, dx)
        g_plane(to).wait_send()
        for pair in range(2):
            x_plane(pair, to).wait_send()
    for dz in range(1, NZ):
        g_line(lax.rem(z + dz, NZ), z).wait_send()
    w_pass.wait_send()
    to_core(0).wait_send()
    to_core(1).wait_send()
    z_copy.wait_send()
    swap_state.wait_sent()
    swap_grad.wait_first()
    swap_grad.wait_sent()
    for store in stores:
        store.wait()


def expert_update(tokens, routes, grads, owner, moves, w_shard, m_shard, v_shard, residual):
    tok_rows, feats = tokens.shape
    hidden = grads.shape[1]
    count = owner.shape[0]
    shard_rows = w_shard.shape[0]
    rows = count * CAP
    dma = pltpu.SemaphoreType.DMA
    vmem = pl.BlockSpec(memory_space=pltpu.VMEM)
    hbm = pl.BlockSpec(memory_space=pl.ANY)
    pair = jnp.stack([moves[1, 1], moves[0, 1]])
    spots = jnp.stack([pair // (NX * NZ), (pair // NZ) % NX, pair % NZ], axis=1)
    places = jnp.concatenate([pair, spots.reshape(-1)])
    return pl.pallas_call(
        kernel,
        out_shape=[jax.ShapeDtypeStruct((shard_rows, hidden), BF16)] * 3,
        in_specs=[
            pl.BlockSpec(memory_space=pltpu.SMEM), vmem, vmem, vmem, hbm, vmem, hbm, hbm, hbm, hbm
        ],
        out_specs=[hbm] * 3,
        scratch_shapes=[
            pltpu.VMEM((NZ, TOP, tok_rows), jnp.int32),
            pltpu.VMEM((NZ, tok_rows, feats), BF16),
            pltpu.VMEM((2, rows // 2, feats), BF16),
            pltpu.VMEM((rows, feats), BF16),
            pltpu.VMEM((PLANE, NZ, CAP, hidden), BF16),
            pltpu.VMEM((PLANE, NZ, CAP, hidden), BF16),
            pltpu.VMEM((NZ, PLANE, CAP, hidden), BF16),
            pltpu.VMEM((feats, hidden), BF16),
            pltpu.VMEM((max(rows // 4, shard_rows), hidden), F32),
            pltpu.VMEM((rows, hidden), BF16),
            pltpu.VMEM((4, shard_rows, hidden), BF16),
            pltpu.VMEM((2, shard_rows, hidden), BF16),
            pltpu.VMEM((shard_rows, hidden), BF16),
            pltpu.VMEM((shard_rows, hidden), BF16),
            dma((9,)),
            dma((NZ,)), dma((NZ,)), dma((NZ,)), dma((NZ,)), dma((NZ,)), dma((NZ,)),
            dma((2, PLANE)), dma((2, PLANE)), dma((PLANE,)), dma((PLANE,)), dma((NZ,)), dma((NZ,)),
            dma((3,)), dma((3,)), dma((3,)), dma((3,)),
            pltpu.VMEM((feats, hidden), BF16),
            pltpu.VMEM((3, shard_rows, hidden), BF16),
            pltpu.VMEM((1, shard_rows, hidden), BF16),
            *swap_scratch(3, shard_rows, hidden),
            *swap_scratch(1, shard_rows, hidden),
        ],
        compiler_params=pltpu.CompilerParams(
            collective_id=0, has_side_effects=True, vmem_limit_bytes=62 * 2**20
        ),
        name="expert_update",
    )(
        places, routes.T, routes.reshape(1, -1), owner[:, None], tokens, grads, w_shard, m_shard, v_shard, residual
    )


def shards(tokens, routes, grad_act, owner, moves, weight, first_moment, second_moment, residual):
    hidden = grad_act.shape[2]
    new_w, new_m, new_v = expert_update(
        tokens, routes, grad_act.reshape(-1, hidden), owner, moves, weight[0], first_moment[0], second_moment[0],
        residual[0, 0],
    )
    return (new_w[None], new_m[None], new_v[None])


def solution(mesh):
    return jax.shard_map(
        shards,
        mesh=mesh,
        in_specs=(
            P(("dp", "expert"), None),
            P(("dp", "expert"), None),
            P(("dp", "expert"), None, None),
            P(),
            P(),
            P("expert", "dp", None),
            P("expert", "dp", None),
            P("expert", "dp", None),
            P("dp", "expert", None, None),
        ),
        out_specs=(P("expert", "dp", None), P("expert", "dp", None), P("expert", "dp", None)),
        check_vma=False,
    )
```

```python
import functools

import jax
import jax.numpy as jnp
from jax import lax
from jax.experimental import pallas as pl
from jax.experimental.pallas import tpu as pltpu
from jax.sharding import PartitionSpec as P

MESH = pl.DeviceIdType.MESH
F32 = jnp.float32
BF16 = jnp.bfloat16

beta_one = 0.9
beta_two = 0.95
step_size = 0.05
epsilon = 1e-08

NY, NX, NZ = 4, 4, 4
PLANE = NY * NX
CAP = 24
TOP = 8


def silu_slope(values):
    sigma = jax.nn.sigmoid(values)
    return sigma * (1.0 + values * (1.0 - sigma))


class Swap:
    def __init__(self, src, pair, spot, at, remote, scratch):
        (self.got1, self.out2, self.got2, self.out3, self.got3, self.out4, self.got4, self.back, self.got,
         self.sent, self.come) = scratch
        self.src, self.pair, self.at, self.remote = src, pair, at, remote
        self.y, self.x, self.z = spot
        self.ys = [p // (NX * NZ) for p in pair]
        self.xs = [(p // NZ) % NX for p in pair]
        self.zs = [p % NZ for p in pair]
        self.half = src.shape[1] // 2
        self.piece = self.half // 4
        self.small = self.piece // 4

    def axes(self, half):
        along = [(self.x, self.xs), (self.y, self.ys)]
        return along if half == 0 else along[::-1]

    def peer(self, half, first, d):
        if first == (half == 0):
            to = lax.rem(self.x + d, NX)
            return to, self.at(self.y * NX + to, self.z), self.x
        to = lax.rem(self.y + d, NY)
        return to, self.at(to * NX + self.x, self.z), self.y

    def rows1(self, half, to):
        return pl.ds(pl.multiple_of(half * self.half + to * self.piece, 16), self.piece)

    def rows2(self, to):
        return pl.ds(pl.multiple_of(to * self.small, 16), self.small)

    def copy1(self, half, d, arriving=False):
        to, device, mine = self.peer(half, True, d)
        return self.remote(self.src.at[:, self.rows1(half, to)], self.got1.at[half, to if arriving else mine],
                           self.sent.at[0, half, to], self.come.at[0, half, to if arriving else mine], device)

    def copy2(self, half, d, arriving=False):
        to, device, mine = self.peer(half, False, d)
        return self.remote(self.out2.at[half, :, self.rows2(to)], self.got2.at[half, to if arriving else mine],
                           self.sent.at[1, half, to], self.come.at[1, half, to if arriving else mine], device)

    def copy3(self, half, d, arriving=False):
        to = lax.rem(self.z + d, NZ)
        device = self.at(self.y * NX + self.x, to)
        mine = to if arriving else self.z
        return self.remote(self.out3.at[half], self.got3.at[half, mine],
                           self.sent.at[2, half, to], self.come.at[2, half, mine], device)

    def copy4(self, half, d, arriving=False):
        to, device, mine = self.peer(half, False, d)
        return self.remote(self.out4.at[half, to], self.got4.at[half, to if arriving else mine],
                           self.sent.at[3, half, to], self.come.at[3, half, to if arriving else mine], device)

    def copy5(self, half, d, arriving=False):
        to, device, mine = self.peer(half, True, d)
        return self.remote(self.back.at[half, to], self.got.at[:, self.rows1(half, to if arriving else mine)],
                           self.sent.at[4, half, to], self.come.at[4, half, to if arriving else mine], device)

    def each(self, act):
        for d in (1, 3, 2):
            for half in range(2):
                act(half, d)

    def start(self):
        self.each(lambda half, d: self.copy1(half, d).start())
        for half in range(2):
            mine = self.peer(half, True, 0)[0]
            self.got1[half, mine] = self.src[:, self.rows1(half, mine), :]

    def second(self):
        self.each(lambda half, d: self.copy1(half, d, True).wait_recv())
        for half in range(2):
            (_, firsts), (second, seconds) = self.axes(half)
            held = (second == seconds[0]) & (self.z == self.zs[0])
            self.out2[half] = self.got1[half, jnp.where(held, firsts[0], firsts[1])]
        self.each(lambda half, d: self.copy2(half, d).start())
        for half in range(2):
            mine = self.peer(half, False, 0)[0]
            self.got2[half, mine] = self.out2[half, :, self.rows2(mine), :]

    def along_z(self):
        self.each(lambda half, d: self.copy2(half, d, True).wait_recv())
        for half in range(2):
            seconds = self.axes(half)[1][1]
            self.out3[half] = self.got2[half, jnp.where(self.z == self.zs[0], seconds[0], seconds[1])]
        self.each(lambda half, d: self.copy3(half, d).start())
        for half in range(2):
            self.got3[half, self.z] = self.out3[half]

    def fourth(self):
        self.each(lambda half, d: self.copy3(half, d, True).wait_recv())
        plane = self.zs[0] == self.zs[1]
        for d in (1, 3, 2, 0):
            for half in range(2):
                seconds = self.axes(half)[1][1]
                to = self.peer(half, False, d)[0]
                takes = (to == seconds[1]) & (self.z == self.zs[1])
                kept = jnp.where(
                    plane,
                    self.got2[half, jnp.where(takes, seconds[0], seconds[1])],
                    self.got3[half, jnp.where(takes, self.zs[0], self.zs[1])],
                )
                if d:
                    self.out4[half, to] = kept
                    self.copy4(half, d).start()
                else:
                    self.got4[half, to] = kept

    def last(self):
        self.each(lambda half, d: self.copy4(half, d, True).wait_recv())
        for d in (1, 3, 2, 0):
            for half in range(2):
                (_, firsts), (_, seconds) = self.axes(half)
                row = (seconds[0] == seconds[1]) & (self.zs[0] == self.zs[1])
                to, device, _ = self.peer(half, True, d)
                index = jnp.where(self.pair[1] == device[1], firsts[0], firsts[1])
                for i in range(4):
                    rows = pl.ds(i * self.small, self.small)
                    part = jnp.where(row, self.got1[half, index, :, rows, :], self.got4[half, i])
                    if d:
                        self.back[half, to, :, rows, :] = part
                    else:
                        first = pl.multiple_of(half * self.half + to * self.piece + i * self.small, 16)
                        self.got[:, pl.ds(first, self.small), :] = part
                if d:
                    self.copy5(half, d).start()

    def wait_last(self):
        self.each(lambda half, d: self.copy5(half, d, True).wait_recv())

    def wait_first(self):
        self.each(lambda half, d: self.copy1(half, d).wait_send())

    def wait_sent(self):
        for copy in (self.copy2, self.copy3, self.copy4, self.copy5):
            self.each(lambda half, d: copy(half, d).wait_send())


class Route:
    def __init__(self, spot, at, remote, send, relay, own, passed, dest, sems):
        self.y, self.x, self.z = spot
        self.at, self.remote = at, remote
        self.send, self.relay, self.own, self.passed, self.dest = send, relay, own, passed, dest
        self.sent1, self.got1, self.sent2, self.got2, self.local = sems

    def spots(self, half):
        return (self.x, self.y) if half == 0 else (self.y, self.x)

    def device(self, half, first, to):
        along_x = first == (half == 0)
        return self.at(self.y * NX + to if along_x else to * NX + self.x, self.z)

    def hop1(self, half, d, arriving=False):
        mine = self.spots(half)[0]
        to = lax.rem(mine + d, 4)
        index = to if arriving else mine
        return self.remote(self.send(half, to), self.relay(half, index), self.sent1.at[half, to],
                           self.got1.at[half, index], self.device(half, True, to))

    def hop2(self, half, d, e, arriving=False):
        first, second = self.spots(half)
        come = lax.rem(first + d, 4)
        to = lax.rem(second + e, 4)
        piece = self.passed(half, come, to) if d else self.own(half, to)
        if not e:
            return pltpu.make_async_copy(piece, self.dest(half, come, second), self.local.at[half, come])
        index = to if arriving else second
        return self.remote(piece, self.dest(half, come, index), self.sent2.at[half, come, to],
                           self.got2.at[half, come, index], self.device(half, False, to))

    def start(self):
        for d in (1, 3, 2):
            for half in range(2):
                self.hop1(half, d).start()
        self.pass_on(0)

    def pass_on(self, d):
        for half in range(2):
            if d:
                self.hop1(half, d, True).wait_recv()
            for e in (1, 3, 2, 0):
                self.hop2(half, d, e).start()

    def relay_all(self):
        for d in (1, 3, 2):
            self.pass_on(d)

    def wait_all(self):
        for half in range(2):
            for d in range(4):
                for e in range(1, 4):
                    self.hop2(half, d, e, True).wait_recv()
                self.hop2(half, d, 0).wait()

    def wait_sent(self):
        for half in range(2):
            for d in range(4):
                if d:
                    self.hop1(half, d).wait_send()
                for e in range(1, 4):
                    self.hop2(half, d, e).wait_send()


def route_sems():
    dma = pltpu.SemaphoreType.DMA
    return [dma((2, 4)), dma((2, 4)), dma((2, 4, 4)), dma((2, 4, 4)), dma((2, 4))]


def swap_scratch(parts, rows, hidden):
    piece, small = rows // 8, rows // 32
    return [
        pltpu.VMEM((2, 4, parts, piece, hidden), BF16),
        pltpu.VMEM((2, parts, piece, hidden), BF16),
        pltpu.VMEM((2, 4, parts, small, hidden), BF16),
        pltpu.VMEM((2, parts, small, hidden), BF16),
        pltpu.VMEM((2, 4, parts, small, hidden), BF16),
        pltpu.VMEM((2, 4, parts, small, hidden), BF16),
        pltpu.VMEM((2, 4, parts, small, hidden), BF16),
        pltpu.VMEM((2, 4, parts, piece, hidden), BF16),
        pltpu.VMEM((parts, rows, hidden), BF16),
        pltpu.SemaphoreType.DMA((5, 2, 4)),
        pltpu.SemaphoreType.DMA((5, 2, 4)),
    ]


def kernel(
    moves, routes_t, owner_row, tokens, grads, w_shard, m_shard, v_shard, residual,
    w_out, m_out, v_out,
    codes, all_tokens, packed_x, relay_x, rows_x, packed_g, passed_g, relay_g, rows_g, w_full, pre, slopes,
    term, pair_got, z_send, z_got,
    local_sem, tok_up, tok_dn, tok_got, code_up, code_dn, code_got,
    gz_sent, gz_got, w_sent, w_got, t_sent, t_got,
    state, grad_small, *rest,
):
    count = owner_row.shape[1]
    tok_rows, feats = tokens.shape
    hidden = grads.shape[1]
    pairs = grads.shape[0]
    shard_rows = w_shard.shape[0]
    scale = float(feats) ** -0.5

    dp = lax.axis_index("dp")
    me = lax.axis_index("expert")
    z_hi, core = dp // 2, dp % 2
    yx, z = me // NZ, me % NZ
    y, x = yx // NX, yx % NX

    def at(yx_to, z_to):
        return (dp, yx_to * NZ + z_to)

    core_peer = (z_hi * 2 + 1 - core, me)
    far_peer = ((1 - z_hi) * 2 + core, me)

    def remote(src, dst, sent, got, to):
        return pltpu.make_async_remote_copy(
            src_ref=src, dst_ref=dst, send_sem=sent, recv_sem=got, device_id=to, device_id_type=MESH
        )

    held_grads = slopes.at[pl.ds(0, pairs)]
    loads = [
        pltpu.make_async_copy(tokens, all_tokens.at[z], local_sem.at[4]),
        pltpu.make_async_copy(w_shard, state.at[0], local_sem.at[5]),
        pltpu.make_async_copy(m_shard, state.at[1], local_sem.at[6]),
        pltpu.make_async_copy(v_shard, state.at[2], local_sem.at[7]),
        pltpu.make_async_copy(residual, term, local_sem.at[8]),
        pltpu.make_async_copy(grads, held_grads, local_sem.at[9]),
    ]
    for load in loads:
        load.start()

    barrier = pltpu.get_barrier_semaphore()
    for d in range(1, 4):
        pl.semaphore_signal(barrier, inc=1, device_id=at(y * NX + lax.rem(x + d, NX), z), device_id_type=MESH)
        pl.semaphore_signal(barrier, inc=1, device_id=at(lax.rem(y + d, NY) * NX + x, z), device_id_type=MESH)
    for dz in range(1, NZ):
        pl.semaphore_signal(barrier, inc=1, device_id=at(yx, lax.rem(z + dz, NZ)), device_id_type=MESH)
    pl.semaphore_signal(barrier, inc=1, device_id=core_peer, device_id_type=MESH)
    pl.semaphore_signal(barrier, inc=1, device_id=far_peer, device_id_type=MESH)
    pl.semaphore_wait(barrier, 3 + 3 + NZ - 1 + 2)

    device_col = lax.broadcasted_iota(jnp.int32, (count, 1), 0)
    expert = lax.broadcasted_iota(jnp.int32, (count, count), 0) == lax.broadcasted_iota(jnp.int32, (count, count), 1)
    owner_col = jnp.sum(jnp.where(expert, owner_row[...], 0), axis=1, keepdims=True)
    before = (
        lax.broadcasted_iota(jnp.int32, (tok_rows, tok_rows), 0)
        < lax.broadcasted_iota(jnp.int32, (tok_rows, tok_rows), 1)
    ).astype(F32).astype(BF16)
    row_targets = [
        jnp.sum(jnp.where(device_col == routes_t[k : k + 1, :], owner_col, 0), axis=0, keepdims=True)
        for k in range(TOP)
    ]
    hits = [jnp.where(device_col == target, 1.0, 0.0) for target in row_targets]
    ranks = jnp.dot(sum(hits).astype(BF16), before, preferred_element_type=F32)
    target = jnp.concatenate(row_targets, axis=0)
    rank = jnp.concatenate([jnp.sum(hit * ranks, axis=0, keepdims=True) for hit in hits], axis=0)
    codes[z] = target * CAP + rank.astype(jnp.int32)
    loads[0].wait()

    def hop(source, up):
        step = 1 if up else -1
        to = at(yx, z + step)
        sems = (tok_up, code_up) if up else (tok_dn, code_dn)
        return (
            remote(all_tokens.at[source], all_tokens.at[source], sems[0].at[source], tok_got.at[source], to),
            remote(codes.at[source], codes.at[source], sems[1].at[source], code_got.at[source], to),
        )

    def send_hop(source):
        @pl.when((source <= z) & (z < NZ - 1))
        def _():
            for copy in hop(source, True):
                copy.start()

        @pl.when((source >= z) & (z > 0))
        def _():
            for copy in hop(source, False):
                copy.start()

    def wait_hop(source, up):
        for copy in hop(source, up):
            copy.wait_recv()

    send_hop(z)

    spread = (
        lax.broadcasted_iota(jnp.int32, (tok_rows, pairs), 0)
        == lax.broadcasted_iota(jnp.int32, (tok_rows, pairs), 1) // TOP
    ).astype(F32).astype(BF16)
    slot_of = lax.broadcasted_iota(jnp.int32, (TOP, pairs), 0) == lax.broadcasted_iota(jnp.int32, (TOP, pairs), 1) % TOP
    flat_target, flat_rank = [
        jnp.sum(
            jnp.where(slot_of, jnp.dot(v.astype(BF16), spread, preferred_element_type=F32), 0.0), axis=0, keepdims=True
        )
        for v in (target.astype(F32), rank)
    ]
    flat_codes = (flat_target * CAP + flat_rank).astype(jnp.int32)

    group = NX * NZ * CAP

    spot = (y, x, z)
    n_sems = len(route_sems())
    route_g = Route(
        spot, at, remote,
        lambda half, to: packed_g.at[to, :, pl.ds(2, 2)] if half else packed_g.at[:, to, pl.ds(0, 2)],
        lambda half, come: passed_g.at[half, come],
        lambda half, to: packed_g.at[y, to, pl.ds(2, 2)] if half else packed_g.at[to, x, pl.ds(0, 2)],
        lambda half, come, to: passed_g.at[half, come, to],
        lambda half, first, second: (
            relay_g.at[first, second, pl.ds(2, 2)] if half else relay_g.at[second, first, pl.ds(0, 2)]
        ),
        rest[:n_sems],
    )
    loads[5].wait()
    for y_to in range(NY):
        slot = lax.broadcasted_iota(jnp.int32, (group, pairs), 0) + y_to * group
        pick = jnp.where(slot == flat_codes, 1.0, 0.0).astype(BF16)
        got = jnp.dot(pick, held_grads[...], preferred_element_type=F32)
        for x_to in range(NX):
            for z_to in range(NZ):
                first = (x_to * NZ + z_to) * CAP
                packed_g[y_to, x_to, z_to] = got[first : first + CAP].astype(BF16)
    route_g.start()

    block = 2 * CAP

    wide = feats // 2

    def pair_route(pair, sems):
        def cols(half):
            return pl.ds(half * wide, wide)

        def rows_of(half, first, second):
            src = first * NX + second if half else second * NX + first
            return rows_x.at[pl.ds(pl.multiple_of((pair * PLANE + src) * block, 16), block), cols(half)]

        return Route(
            spot, at, remote,
            lambda half, to: (
                packed_x.at[pair, to, :, :, cols(half)] if half else packed_x.at[pair, :, to, :, cols(half)]
            ),
            lambda half, come: relay_x.at[pair, half, come],
            lambda half, to: (
                packed_x.at[pair, y, to, :, cols(half)] if half else packed_x.at[pair, to, x, :, cols(half)]
            ),
            lambda half, come, to: relay_x.at[pair, half, come, to],
            rows_of,
            sems,
        )

    def pack_pair(pair, route):
        part = NX * block
        s = lax.broadcasted_iota(jnp.int32, (part, tok_rows), 0)
        to = (s * 1366) >> 16
        half = (s * 2731) >> 16
        rank = s - half * CAP
        for y_to in range(NY):
            want = ((y_to * NX + to) * NZ + z) * CAP + rank
            picks = []
            for sub in range(2):
                source = codes[pair * 2 + sub]
                mine = jnp.where(half == 2 * to + sub, want, -1)
                hit = mine == source[0:1, :]
                for k in range(1, TOP):
                    hit = hit | (mine == source[k : k + 1, :])
                picks.append(jnp.where(hit, 1.0, 0.0).astype(BF16))
            pick = jnp.concatenate(picks, axis=1)
            for c in range(2):
                both = all_tokens[pl.ds(pair * 2, 2), :, pl.ds(c * wide, wide)].reshape(2 * tok_rows, wide)
                got = jnp.dot(pick, both, preferred_element_type=F32).astype(BF16)
                packed_x[pair, y_to, :, :, pl.ds(c * wide, wide)] = got.reshape(NX, block, wide)
        route.start()

    def take_hop(distance):
        @pl.when(z >= distance)
        def _():
            wait_hop(z - distance, True)
            send_hop(z - distance)

        @pl.when(z + distance < NZ)
        def _():
            wait_hop(z + distance, False)
            send_hop(z + distance)

    my_pair = z // 2
    route_mine = pair_route(my_pair, rest[n_sems : 2 * n_sems])
    route_other = pair_route(1 - my_pair, rest[2 * n_sems : 3 * n_sems])
    swaps = rest[3 * n_sems :]
    take_hop(1)
    pack_pair(my_pair, route_mine)
    take_hop(2)

    def w_rows(owner_dp):
        return w_full.at[pl.ds(pl.multiple_of(owner_dp * shard_rows, 16), shard_rows)]

    for load in loads[1:4]:
        load.wait()
    w_full[pl.ds(pl.multiple_of(dp * shard_rows, 16), shard_rows), :] = state[0]
    far_dp = (1 - z_hi) * 2 + core
    near_dp = z_hi * 2 + 1 - core
    w_far = remote(state.at[0], w_rows(dp), w_sent.at[0], w_got.at[0], far_peer)
    w_near = remote(state.at[0], w_rows(dp), w_sent.at[1], w_got.at[1], core_peer)
    w_pass = remote(w_rows(far_dp), w_rows(far_dp), w_sent.at[2], w_got.at[2], core_peer)
    w_far.start()
    w_near.start()

    route_g.relay_all()
    take_hop(3)
    pack_pair(1 - my_pair, route_other)
    route_mine.relay_all()

    pair = (moves[1, 1], moves[0, 1])
    half_swap = len(swaps) // 2
    swap_state = Swap(state, pair, (y, x, z), at, remote, swaps[:half_swap])
    swap_grad = Swap(grad_small, pair, (y, x, z), at, remote, swaps[half_swap:])

    route_g.wait_all()

    def g_line(z_to, z_from):
        return remote(relay_g.at[:, :, z_to], rows_g.at[z_from], gz_sent.at[z_to], gz_got.at[z_from], at(yx, z_to))

    for dz in range(1, NZ):
        g_line(lax.rem(z + dz, NZ), z).start()
    self_rows = pltpu.make_async_copy(relay_g.at[:, :, z], rows_g.at[z], local_sem.at[3])
    self_rows.start()
    route_other.relay_all()
    swap_state.start()

    w_far.wait_recv()
    w_pass.start()
    w_near.wait_recv()
    w_pass.wait_recv()

    def wait_line(z_from):
        remote(
            relay_g.at[:, :, z_from], rows_g.at[z_from], gz_sent.at[z_from], gz_got.at[z_from], at(yx, z_from)
        ).wait_recv()

    def forward(pair):
        per = PLANE // 2
        for part in range(2):
            base = pl.multiple_of((pair * PLANE + part * per) * block, 16)
            pre[pl.ds(0, per * block), :] = jnp.dot(
                rows_x[pl.ds(base, per * block), :], w_full[...], preferred_element_type=F32
            ) * scale

            def body(i, _):
                rows = pl.ds(pl.multiple_of(i * block, 16), block)
                src_y, src_x = part * (per // NX) + i // NX, i % NX
                g = jnp.concatenate(
                    [rows_g[pair * 2, src_y, src_x].astype(F32), rows_g[pair * 2 + 1, src_y, src_x].astype(F32)], axis=0
                )
                slope = (g * silu_slope(pre[rows, :])).astype(BF16)
                slopes[pl.ds(pl.multiple_of(base + i * block, 16), block), :] = slope
                return 0

            lax.fori_loop(0, per, body, 0)

    route_mine.wait_all()
    self_rows.wait()
    wait_line(my_pair * 4 + 1 - z)
    forward(my_pair)
    swap_state.second()
    route_other.wait_all()
    for sub in range(2):
        wait_line((1 - my_pair) * 2 + sub)
    forward(1 - my_pair)
    swap_state.along_z()

    tile = shard_rows // 2

    def gradient(shard):
        def body(i, _):
            first = pl.multiple_of(shard * shard_rows + i * tile, 128)
            part = lax.dot_general(
                rows_x[:, pl.ds(first, tile)], slopes[...], (((0,), (0,)), ((), ())),
                preferred_element_type=F32,
            )
            rows = pl.ds(pl.multiple_of(i * tile, 16), tile)
            term[shard, rows, :] = (part * scale + term[shard, rows, :].astype(F32)).astype(BF16)
            return 0

        lax.fori_loop(0, 2, body, 0)

    def to_core(z_hi_of):
        shard = z_hi_of * 2 + 1 - core
        return remote(term.at[shard], pair_got.at[z_hi_of], t_sent.at[z_hi_of], t_got.at[z_hi_of], core_peer)

    loads[4].wait()
    gradient(far_dp + 1 - 2 * core)
    to_core(1 - z_hi).start()
    gradient(far_dp)
    to_core(1 - z_hi).wait_recv()
    z_send[...] = (term[far_dp].astype(F32) + pair_got[1 - z_hi].astype(F32)).astype(BF16)
    z_copy = remote(z_send, z_got, t_sent.at[2], t_got.at[2], far_peer)
    z_copy.start()
    gradient(near_dp)
    to_core(z_hi).start()
    swap_state.fourth()
    gradient(dp)
    swap_state.last()
    to_core(z_hi).wait_recv()
    z_copy.wait_recv()
    grad_total = pre
    grad_total[pl.ds(0, shard_rows), :] = term[dp].astype(F32) + pair_got[z_hi].astype(F32) + z_got[...].astype(F32)
    grad_small[0] = grad_total[pl.ds(0, shard_rows), :].astype(BF16)

    swap_grad.start()
    swap_grad.second()
    swap_grad.along_z()
    swap_grad.fourth()
    swap_grad.last()
    swap_state.wait_last()
    swap_grad.wait_last()

    swap_state.wait_first()
    w_far.wait_send()
    w_near.wait_send()
    moved = (pair[0] == me) | (pair[1] == me)

    def update(i, _):
        rows = pl.ds(pl.multiple_of(i * 64, 16), 64)
        total = jnp.where(moved, swap_grad.got[0, rows, :].astype(F32), grad_total[rows, :])
        old = [
            jnp.where(moved, swap_state.got[c, rows, :].astype(F32), state[c, rows, :].astype(F32))
            for c in range(3)
        ]
        moment_one = beta_one * old[1] + (1.0 - beta_one) * total
        moment_two = beta_two * old[2] + (1.0 - beta_two) * total * total
        state[0, rows, :] = (old[0] - step_size * moment_one / (jnp.sqrt(moment_two) + epsilon)).astype(BF16)
        state[1, rows, :] = moment_one.astype(BF16)
        state[2, rows, :] = moment_two.astype(BF16)
        return 0

    lax.fori_loop(0, shard_rows // 64, update, 0)
    stores = [
        pltpu.make_async_copy(state.at[c], out, local_sem.at[5 + c]) for c, out in enumerate((w_out, m_out, v_out))
    ]
    for store in stores:
        store.start()

    for source in range(NZ):

        @pl.when((source <= z) & (z < NZ - 1))
        def _():
            for copy in hop(source, True):
                copy.wait_send()

        @pl.when((source >= z) & (z > 0))
        def _():
            for copy in hop(source, False):
                copy.wait_send()

    for route in (route_g, route_mine, route_other):
        route.wait_sent()
    for dz in range(1, NZ):
        g_line(lax.rem(z + dz, NZ), z).wait_send()
    w_pass.wait_send()
    to_core(0).wait_send()
    to_core(1).wait_send()
    z_copy.wait_send()
    swap_state.wait_sent()
    swap_grad.wait_first()
    swap_grad.wait_sent()
    for store in stores:
        store.wait()


def expert_update(tokens, routes, grads, owner, moves, w_shard, m_shard, v_shard, residual):
    tok_rows, feats = tokens.shape
    hidden = grads.shape[1]
    count = owner.shape[0]
    shard_rows = w_shard.shape[0]
    rows = count * CAP
    dma = pltpu.SemaphoreType.DMA
    vmem = pl.BlockSpec(memory_space=pltpu.VMEM)
    hbm = pl.BlockSpec(memory_space=pl.ANY)
    return pl.pallas_call(
        kernel,
        out_shape=[jax.ShapeDtypeStruct((shard_rows, hidden), BF16)] * 3,
        in_specs=[
            pl.BlockSpec(memory_space=pltpu.SMEM), vmem, vmem, hbm, hbm, hbm, hbm, hbm, hbm
        ],
        out_specs=[hbm] * 3,
        scratch_shapes=[
            pltpu.VMEM((NZ, TOP, tok_rows), jnp.int32),
            pltpu.VMEM((NZ, tok_rows, feats), BF16),
            pltpu.VMEM((2, NY, NX, 2 * CAP, feats), BF16),
            pltpu.VMEM((2, 2, 4, 4, 2 * CAP, feats // 2), BF16),
            pltpu.VMEM((rows, feats), BF16),
            pltpu.VMEM((NY, NX, NZ, CAP, hidden), BF16),
            pltpu.VMEM((2, 4, 4, 2, CAP, hidden), BF16),
            pltpu.VMEM((NY, NX, NZ, CAP, hidden), BF16),
            pltpu.VMEM((NZ, NY, NX, CAP, hidden), BF16),
            pltpu.VMEM((feats, hidden), BF16),
            pltpu.VMEM((max(rows // 4, shard_rows), hidden), F32),
            pltpu.VMEM((rows, hidden), BF16),
            pltpu.VMEM((4, shard_rows, hidden), BF16),
            pltpu.VMEM((2, shard_rows, hidden), BF16),
            pltpu.VMEM((shard_rows, hidden), BF16),
            pltpu.VMEM((shard_rows, hidden), BF16),
            dma((10,)),
            dma((NZ,)), dma((NZ,)), dma((NZ,)), dma((NZ,)), dma((NZ,)), dma((NZ,)),
            dma((NZ,)), dma((NZ,)),
            dma((3,)), dma((3,)), dma((3,)), dma((3,)),
            pltpu.VMEM((3, shard_rows, hidden), BF16),
            pltpu.VMEM((1, shard_rows, hidden), BF16),
            *route_sems(), *route_sems(), *route_sems(),
            *swap_scratch(3, shard_rows, hidden),
            *swap_scratch(1, shard_rows, hidden),
        ],
        compiler_params=pltpu.CompilerParams(
            collective_id=0, has_side_effects=True, vmem_limit_bytes=62 * 2**20
        ),
        name="expert_update",
    )(
        moves, routes.T, owner[None, :], tokens, grads, w_shard, m_shard, v_shard,
        residual.reshape(-1, shard_rows, hidden),
    )


def shards(tokens, routes, grad_act, owner, moves, weight, first_moment, second_moment, residual):
    hidden = grad_act.shape[2]
    new_w, new_m, new_v = expert_update(
        tokens, routes, grad_act.reshape(-1, hidden), owner, moves, weight[0], first_moment[0], second_moment[0],
        residual[0, 0],
    )
    return (new_w[None], new_m[None], new_v[None])


def solution(mesh):
    return jax.shard_map(
        shards,
        mesh=mesh,
        in_specs=(
            P(("dp", "expert"), None),
            P(("dp", "expert"), None),
            P(("dp", "expert"), None, None),
            P(),
            P(),
            P("expert", "dp", None),
            P("expert", "dp", None),
            P("expert", "dp", None),
            P("dp", "expert", None, None),
        ),
        out_specs=(P("expert", "dp", None), P("expert", "dp", None), P("expert", "dp", None)),
        check_vma=False,
    )
```

```python
import functools

import jax
import jax.numpy as jnp
from jax import lax
from jax.experimental import pallas as pl
from jax.experimental.pallas import tpu as pltpu
from jax.sharding import PartitionSpec as P

MESH = pl.DeviceIdType.MESH
F32 = jnp.float32
BF16 = jnp.bfloat16

beta_one = 0.9
beta_two = 0.95
step_size = 0.05
epsilon = 1e-08

NY, NX, NZ = 4, 4, 4
PLANE = NY * NX
CAP = 24
TOP = 8


def silu_slope(values):
    sigma = jax.nn.sigmoid(values)
    return sigma * (1.0 + values * (1.0 - sigma))


class Swap:
    def __init__(self, src, pair, spot, at, remote, scratch):
        (self.got1, self.out2, self.got2, self.out3, self.got3, self.out4, self.got4, self.back, self.got,
         self.sent, self.come) = scratch
        self.src, self.pair, self.at, self.remote = src, pair, at, remote
        self.y, self.x, self.z = spot
        self.ys = [p // (NX * NZ) for p in pair]
        self.xs = [(p // NZ) % NX for p in pair]
        self.zs = [p % NZ for p in pair]
        self.half = src.shape[1] // 2
        self.piece = self.half // 4
        self.small = self.piece // 4

    def axes(self, half):
        along = [(self.x, self.xs), (self.y, self.ys)]
        return along if half == 0 else along[::-1]

    def peer(self, half, first, d):
        if first == (half == 0):
            to = lax.rem(self.x + d, NX)
            return to, self.at(self.y * NX + to, self.z), self.x
        to = lax.rem(self.y + d, NY)
        return to, self.at(to * NX + self.x, self.z), self.y

    def rows1(self, half, to):
        return pl.ds(pl.multiple_of(half * self.half + to * self.piece, 16), self.piece)

    def rows2(self, to):
        return pl.ds(pl.multiple_of(to * self.small, 16), self.small)

    def copy1(self, half, d, arriving=False):
        to, device, mine = self.peer(half, True, d)
        return self.remote(self.src.at[:, self.rows1(half, to)], self.got1.at[half, to if arriving else mine],
                           self.sent.at[0, half, to], self.come.at[0, half, to if arriving else mine], device)

    def copy2(self, half, d, arriving=False):
        to, device, mine = self.peer(half, False, d)
        return self.remote(self.out2.at[half, :, self.rows2(to)], self.got2.at[half, to if arriving else mine],
                           self.sent.at[1, half, to], self.come.at[1, half, to if arriving else mine], device)

    def copy3(self, half, d, arriving=False):
        to = lax.rem(self.z + d, NZ)
        device = self.at(self.y * NX + self.x, to)
        mine = to if arriving else self.z
        return self.remote(self.out3.at[half], self.got3.at[half, mine],
                           self.sent.at[2, half, to], self.come.at[2, half, mine], device)

    def copy4(self, half, d, arriving=False):
        to, device, mine = self.peer(half, False, d)
        return self.remote(self.out4.at[half, to], self.got4.at[half, to if arriving else mine],
                           self.sent.at[3, half, to], self.come.at[3, half, to if arriving else mine], device)

    def copy5(self, half, d, arriving=False):
        to, device, mine = self.peer(half, True, d)
        return self.remote(self.back.at[half, to], self.got.at[:, self.rows1(half, to if arriving else mine)],
                           self.sent.at[4, half, to], self.come.at[4, half, to if arriving else mine], device)

    def each(self, act):
        for d in (1, 3, 2):
            for half in range(2):
                act(half, d)

    def start(self):
        self.each(lambda half, d: self.copy1(half, d).start())
        for half in range(2):
            mine = self.peer(half, True, 0)[0]
            self.got1[half, mine] = self.src[:, self.rows1(half, mine), :]

    def second(self):
        self.each(lambda half, d: self.copy1(half, d, True).wait_recv())
        for half in range(2):
            (_, firsts), (second, seconds) = self.axes(half)
            held = (second == seconds[0]) & (self.z == self.zs[0])
            self.out2[half] = self.got1[half, jnp.where(held, firsts[0], firsts[1])]
        self.each(lambda half, d: self.copy2(half, d).start())
        for half in range(2):
            mine = self.peer(half, False, 0)[0]
            self.got2[half, mine] = self.out2[half, :, self.rows2(mine), :]

    def along_z(self):
        self.each(lambda half, d: self.copy2(half, d, True).wait_recv())
        for half in range(2):
            seconds = self.axes(half)[1][1]
            self.out3[half] = self.got2[half, jnp.where(self.z == self.zs[0], seconds[0], seconds[1])]
        self.each(lambda half, d: self.copy3(half, d).start())
        for half in range(2):
            self.got3[half, self.z] = self.out3[half]

    def fourth(self):
        self.each(lambda half, d: self.copy3(half, d, True).wait_recv())
        plane = self.zs[0] == self.zs[1]
        for d in (1, 3, 2, 0):
            for half in range(2):
                seconds = self.axes(half)[1][1]
                to = self.peer(half, False, d)[0]
                takes = (to == seconds[1]) & (self.z == self.zs[1])
                kept = jnp.where(
                    plane,
                    self.got2[half, jnp.where(takes, seconds[0], seconds[1])],
                    self.got3[half, jnp.where(takes, self.zs[0], self.zs[1])],
                )
                if d:
                    self.out4[half, to] = kept
                    self.copy4(half, d).start()
                else:
                    self.got4[half, to] = kept

    def last(self):
        self.each(lambda half, d: self.copy4(half, d, True).wait_recv())
        for d in (1, 3, 2, 0):
            for half in range(2):
                (_, firsts), (_, seconds) = self.axes(half)
                row = (seconds[0] == seconds[1]) & (self.zs[0] == self.zs[1])
                to, device, _ = self.peer(half, True, d)
                index = jnp.where(self.pair[1] == device[1], firsts[0], firsts[1])
                for i in range(4):
                    rows = pl.ds(i * self.small, self.small)
                    part = jnp.where(row, self.got1[half, index, :, rows, :], self.got4[half, i])
                    if d:
                        self.back[half, to, :, rows, :] = part
                    else:
                        first = pl.multiple_of(half * self.half + to * self.piece + i * self.small, 16)
                        self.got[:, pl.ds(first, self.small), :] = part
                if d:
                    self.copy5(half, d).start()

    def wait_last(self):
        self.each(lambda half, d: self.copy5(half, d, True).wait_recv())

    def wait_first(self):
        self.each(lambda half, d: self.copy1(half, d).wait_send())

    def wait_sent(self):
        for copy in (self.copy2, self.copy3, self.copy4, self.copy5):
            self.each(lambda half, d: copy(half, d).wait_send())


class Route:
    def __init__(self, spot, at, remote, send, relay, own, passed, dest, sems):
        self.y, self.x, self.z = spot
        self.at, self.remote = at, remote
        self.send, self.relay, self.own, self.passed, self.dest = send, relay, own, passed, dest
        self.sent1, self.got1, self.sent2, self.got2, self.local = sems

    def spots(self, half):
        return (self.x, self.y) if half == 0 else (self.y, self.x)

    def device(self, half, first, to):
        along_x = first == (half == 0)
        return self.at(self.y * NX + to if along_x else to * NX + self.x, self.z)

    def hop1(self, half, d, arriving=False):
        mine = self.spots(half)[0]
        to = lax.rem(mine + d, 4)
        index = to if arriving else mine
        return self.remote(self.send(half, to), self.relay(half, index), self.sent1.at[half, to],
                           self.got1.at[half, index], self.device(half, True, to))

    def hop2(self, half, d, e, arriving=False):
        first, second = self.spots(half)
        come = lax.rem(first + d, 4)
        to = lax.rem(second + e, 4)
        piece = self.passed(half, come, to) if d else self.own(half, to)
        if not e:
            return pltpu.make_async_copy(piece, self.dest(half, come, second), self.local.at[half, come])
        index = to if arriving else second
        return self.remote(piece, self.dest(half, come, index), self.sent2.at[half, come, to],
                           self.got2.at[half, come, index], self.device(half, False, to))

    def start(self):
        for d in (1, 3, 2):
            for half in range(2):
                self.hop1(half, d).start()
        self.pass_on(0)

    def pass_on(self, d):
        for half in range(2):
            if d:
                self.hop1(half, d, True).wait_recv()
            for e in (1, 3, 2, 0):
                self.hop2(half, d, e).start()

    def relay_all(self):
        for d in (1, 3, 2):
            self.pass_on(d)

    def wait_all(self):
        for half in range(2):
            for d in range(4):
                for e in range(1, 4):
                    self.hop2(half, d, e, True).wait_recv()
                self.hop2(half, d, 0).wait()

    def wait_sent(self):
        for half in range(2):
            for d in range(4):
                if d:
                    self.hop1(half, d).wait_send()
                for e in range(1, 4):
                    self.hop2(half, d, e).wait_send()


def route_sems():
    dma = pltpu.SemaphoreType.DMA
    return [dma((2, 4)), dma((2, 4)), dma((2, 4, 4)), dma((2, 4, 4)), dma((2, 4))]


def swap_scratch(parts, rows, hidden):
    piece, small = rows // 8, rows // 32
    return [
        pltpu.VMEM((2, 4, parts, piece, hidden), BF16),
        pltpu.VMEM((2, parts, piece, hidden), BF16),
        pltpu.VMEM((2, 4, parts, small, hidden), BF16),
        pltpu.VMEM((2, parts, small, hidden), BF16),
        pltpu.VMEM((2, 4, parts, small, hidden), BF16),
        pltpu.VMEM((2, 4, parts, small, hidden), BF16),
        pltpu.VMEM((2, 4, parts, small, hidden), BF16),
        pltpu.VMEM((2, 4, parts, piece, hidden), BF16),
        pltpu.VMEM((parts, rows, hidden), BF16),
        pltpu.SemaphoreType.DMA((5, 2, 4)),
        pltpu.SemaphoreType.DMA((5, 2, 4)),
    ]


def kernel(
    moves, routes_t, owner_row, tokens, grads, w_shard, m_shard, v_shard, residual,
    w_out, m_out, v_out,
    codes, all_tokens, packed_x, relay_x, rows_x, packed_g, passed_g, relay_g, rows_g, w_full, pre, slopes,
    term, pair_got, z_send, z_got,
    local_sem, tok_sent, tok_got, code_sent, code_got,
    gz_sent, gz_got, w_sent, w_got, t_sent, t_got,
    state, grad_small, *rest,
):
    count = owner_row.shape[1]
    tok_rows, feats = tokens.shape
    hidden = grads.shape[1]
    pairs = grads.shape[0]
    shard_rows = w_shard.shape[0]
    scale = float(feats) ** -0.5

    dp = lax.axis_index("dp")
    me = lax.axis_index("expert")
    z_hi, core = dp // 2, dp % 2
    yx, z = me // NZ, me % NZ
    y, x = yx // NX, yx % NX

    def at(yx_to, z_to):
        return (dp, yx_to * NZ + z_to)

    turn = 1 - 2 * core

    def ring(step):
        p = lax.rem(z_hi * NZ + z + step + 2 * NZ, 2 * NZ)
        return ((p // NZ) * 2 + core, yx * NZ + p % NZ), p % NZ

    core_peer = (z_hi * 2 + 1 - core, me)
    far_peer = ((1 - z_hi) * 2 + core, me)

    def remote(src, dst, sent, got, to):
        return pltpu.make_async_remote_copy(
            src_ref=src, dst_ref=dst, send_sem=sent, recv_sem=got, device_id=to, device_id_type=MESH
        )

    held_grads = slopes.at[pl.ds(0, pairs)]
    loads = [
        pltpu.make_async_copy(tokens, all_tokens.at[z], local_sem.at[4]),
        pltpu.make_async_copy(w_shard, state.at[0], local_sem.at[5]),
        pltpu.make_async_copy(m_shard, state.at[1], local_sem.at[6]),
        pltpu.make_async_copy(v_shard, state.at[2], local_sem.at[7]),
        pltpu.make_async_copy(residual, term, local_sem.at[8]),
        pltpu.make_async_copy(grads, held_grads, local_sem.at[9]),
    ]
    for load in loads:
        load.start()

    barrier = pltpu.get_barrier_semaphore()
    for d in range(1, 4):
        pl.semaphore_signal(barrier, inc=1, device_id=at(y * NX + lax.rem(x + d, NX), z), device_id_type=MESH)
        pl.semaphore_signal(barrier, inc=1, device_id=at(lax.rem(y + d, NY) * NX + x, z), device_id_type=MESH)
    for dz in range(1, NZ):
        pl.semaphore_signal(barrier, inc=1, device_id=at(yx, lax.rem(z + dz, NZ)), device_id_type=MESH)
    for step in (1, -1, 2, -2):
        pl.semaphore_signal(barrier, inc=1, device_id=ring(step)[0], device_id_type=MESH)
    pl.semaphore_signal(barrier, inc=1, device_id=core_peer, device_id_type=MESH)
    pl.semaphore_signal(barrier, inc=1, device_id=far_peer, device_id_type=MESH)
    pl.semaphore_wait(barrier, 3 + 3 + NZ - 1 + 4 + 2)

    device_col = lax.broadcasted_iota(jnp.int32, (count, 1), 0)
    expert = lax.broadcasted_iota(jnp.int32, (count, count), 0) == lax.broadcasted_iota(jnp.int32, (count, count), 1)
    owner_col = jnp.sum(jnp.where(expert, owner_row[...], 0), axis=1, keepdims=True)
    before = (
        lax.broadcasted_iota(jnp.int32, (tok_rows, tok_rows), 0)
        < lax.broadcasted_iota(jnp.int32, (tok_rows, tok_rows), 1)
    ).astype(F32).astype(BF16)
    row_targets = [
        jnp.sum(jnp.where(device_col == routes_t[k : k + 1, :], owner_col, 0), axis=0, keepdims=True)
        for k in range(TOP)
    ]
    hits = [jnp.where(device_col == target, 1.0, 0.0) for target in row_targets]
    ranks = jnp.dot(sum(hits).astype(BF16), before, preferred_element_type=F32)
    target = jnp.concatenate(row_targets, axis=0)
    rank = jnp.concatenate([jnp.sum(hit * ranks, axis=0, keepdims=True) for hit in hits], axis=0)
    codes[z] = target * CAP + rank.astype(jnp.int32)
    loads[0].wait()

    def hop(source, step, sent):
        to = ring(step)[0]
        return (
            remote(all_tokens.at[source], all_tokens.at[source], tok_sent.at[sent], tok_got.at[source], to),
            remote(codes.at[source], codes.at[source], code_sent.at[sent], code_got.at[source], to),
        )

    behind = ring(-turn)[1]
    hops = hop(z, turn, 0) + hop(z, -turn, 1)
    passed_hop = hop(behind, turn, 2)

    def wait_hop(source):
        for copy in hop(source, 1, 0):
            copy.wait_recv()

    for copy in hops:
        copy.start()

    for load in loads[1:4]:
        load.wait()
    pair = (moves[1, 1], moves[0, 1])
    swaps = rest[3 * len(route_sems()) :]
    half_swap = len(swaps) // 2
    swap_state = Swap(state, pair, (y, x, z), at, remote, swaps[:half_swap])
    swap_grad = Swap(grad_small, pair, (y, x, z), at, remote, swaps[half_swap:])

    swap_state.start()

    spread = (
        lax.broadcasted_iota(jnp.int32, (tok_rows, pairs), 0)
        == lax.broadcasted_iota(jnp.int32, (tok_rows, pairs), 1) // TOP
    ).astype(F32).astype(BF16)
    slot_of = lax.broadcasted_iota(jnp.int32, (TOP, pairs), 0) == lax.broadcasted_iota(jnp.int32, (TOP, pairs), 1) % TOP
    flat_target, flat_rank = [
        jnp.sum(
            jnp.where(slot_of, jnp.dot(v.astype(BF16), spread, preferred_element_type=F32), 0.0), axis=0, keepdims=True
        )
        for v in (target.astype(F32), rank)
    ]
    flat_codes = (flat_target * CAP + flat_rank).astype(jnp.int32)

    group = NX * NZ * CAP

    spot = (y, x, z)
    n_sems = len(route_sems())
    route_g = Route(
        spot, at, remote,
        lambda half, to: packed_g.at[to, :, pl.ds(2, 2)] if half else packed_g.at[:, to, pl.ds(0, 2)],
        lambda half, come: passed_g.at[half, come],
        lambda half, to: packed_g.at[y, to, pl.ds(2, 2)] if half else packed_g.at[to, x, pl.ds(0, 2)],
        lambda half, come, to: passed_g.at[half, come, to],
        lambda half, first, second: (
            relay_g.at[first, second, pl.ds(2, 2)] if half else relay_g.at[second, first, pl.ds(0, 2)]
        ),
        rest[:n_sems],
    )
    loads[5].wait()
    for y_to in range(NY):
        slot = lax.broadcasted_iota(jnp.int32, (group, pairs), 0) + y_to * group
        pick = jnp.where(slot == flat_codes, 1.0, 0.0).astype(BF16)
        got = jnp.dot(pick, held_grads[...], preferred_element_type=F32)
        for x_to in range(NX):
            for z_to in range(NZ):
                first = (x_to * NZ + z_to) * CAP
                packed_g[y_to, x_to, z_to] = got[first : first + CAP].astype(BF16)
    route_g.start()

    block = 2 * CAP

    wide = feats // 2

    def pair_route(pair, sems):
        def cols(half):
            return pl.ds(half * wide, wide)

        def rows_of(half, first, second):
            src = first * NX + second if half else second * NX + first
            return rows_x.at[pl.ds(pl.multiple_of((pair * PLANE + src) * block, 16), block), cols(half)]

        return Route(
            spot, at, remote,
            lambda half, to: (
                packed_x.at[pair, to, :, :, cols(half)] if half else packed_x.at[pair, :, to, :, cols(half)]
            ),
            lambda half, come: relay_x.at[pair, half, come],
            lambda half, to: (
                packed_x.at[pair, y, to, :, cols(half)] if half else packed_x.at[pair, to, x, :, cols(half)]
            ),
            lambda half, come, to: relay_x.at[pair, half, come, to],
            rows_of,
            sems,
        )

    def pack_pair(pair, route):
        part = NX * block
        s = lax.broadcasted_iota(jnp.int32, (part, tok_rows), 0)
        to = (s * 1366) >> 16
        half = (s * 2731) >> 16
        rank = s - half * CAP
        for y_to in range(NY):
            want = ((y_to * NX + to) * NZ + z) * CAP + rank
            picks = []
            for sub in range(2):
                source = codes[pair * 2 + sub]
                mine = jnp.where(half == 2 * to + sub, want, -1)
                hit = mine == source[0:1, :]
                for k in range(1, TOP):
                    hit = hit | (mine == source[k : k + 1, :])
                picks.append(jnp.where(hit, 1.0, 0.0).astype(BF16))
            pick = jnp.concatenate(picks, axis=1)
            for c in range(2):
                both = all_tokens[pl.ds(pair * 2, 2), :, pl.ds(c * wide, wide)].reshape(2 * tok_rows, wide)
                got = jnp.dot(pick, both, preferred_element_type=F32).astype(BF16)
                packed_x[pair, y_to, :, :, pl.ds(c * wide, wide)] = got.reshape(NX, block, wide)
        route.start()

    my_pair = z // 2
    route_mine = pair_route(my_pair, rest[n_sems : 2 * n_sems])
    route_other = pair_route(1 - my_pair, rest[2 * n_sems : 3 * n_sems])
    wait_hop(behind)
    for copy in passed_hop:
        copy.start()
    wait_hop(ring(turn)[1])
    pack_pair(my_pair, route_mine)
    swap_state.second()

    def w_rows(owner_dp):
        return w_full.at[pl.ds(pl.multiple_of(owner_dp * shard_rows, 16), shard_rows)]

    w_full[pl.ds(pl.multiple_of(dp * shard_rows, 16), shard_rows), :] = state[0]
    far_dp = (1 - z_hi) * 2 + core
    near_dp = z_hi * 2 + 1 - core
    w_far = remote(state.at[0], w_rows(dp), w_sent.at[0], w_got.at[0], far_peer)
    w_near = remote(state.at[0], w_rows(dp), w_sent.at[1], w_got.at[1], core_peer)
    w_pass = remote(w_rows(far_dp), w_rows(far_dp), w_sent.at[2], w_got.at[2], core_peer)
    w_far.start()
    w_near.start()

    route_g.relay_all()
    wait_hop(ring(2 * turn)[1])
    pack_pair(1 - my_pair, route_other)
    swap_state.along_z()
    route_mine.relay_all()

    route_g.wait_all()

    def g_line(step):
        device, z_to = ring(step)
        return remote(relay_g.at[:, :, z_to], rows_g.at[z], gz_sent.at[z_to], gz_got.at[z], device)

    g_lines = [g_line(2 * turn), g_line(turn), g_line(-turn)]
    for copy in g_lines:
        copy.start()
    self_rows = pltpu.make_async_copy(relay_g.at[:, :, z], rows_g.at[z], local_sem.at[3])
    self_rows.start()
    route_other.relay_all()
    swap_state.fourth()

    w_far.wait_recv()
    w_pass.start()
    w_near.wait_recv()
    w_pass.wait_recv()

    def wait_line(z_from):
        remote(
            relay_g.at[:, :, z_from], rows_g.at[z_from], gz_sent.at[z_from], gz_got.at[z_from], at(yx, z_from)
        ).wait_recv()

    def forward(pair):
        per = PLANE // 2
        for part in range(2):
            base = pl.multiple_of((pair * PLANE + part * per) * block, 16)
            pre[pl.ds(0, per * block), :] = jnp.dot(
                rows_x[pl.ds(base, per * block), :], w_full[...], preferred_element_type=F32
            ) * scale

            def body(i, _):
                rows = pl.ds(pl.multiple_of(i * block, 16), block)
                src_y, src_x = part * (per // NX) + i // NX, i % NX
                g = jnp.concatenate(
                    [rows_g[pair * 2, src_y, src_x].astype(F32), rows_g[pair * 2 + 1, src_y, src_x].astype(F32)], axis=0
                )
                slope = (g * silu_slope(pre[rows, :])).astype(BF16)
                slopes[pl.ds(pl.multiple_of(base + i * block, 16), block), :] = slope
                return 0

            lax.fori_loop(0, per, body, 0)

    route_mine.wait_all()
    self_rows.wait()
    wait_line(my_pair * 4 + 1 - z)
    forward(my_pair)
    route_other.wait_all()
    for sub in range(2):
        wait_line((1 - my_pair) * 2 + sub)
    forward(1 - my_pair)
    swap_state.last()

    tile = shard_rows // 2

    def gradient(shard):
        def body(i, _):
            first = pl.multiple_of(shard * shard_rows + i * tile, 128)
            part = lax.dot_general(
                rows_x[:, pl.ds(first, tile)], slopes[...], (((0,), (0,)), ((), ())),
                preferred_element_type=F32,
            )
            rows = pl.ds(pl.multiple_of(i * tile, 16), tile)
            term[shard, rows, :] = (part * scale + term[shard, rows, :].astype(F32)).astype(BF16)
            return 0

        lax.fori_loop(0, 2, body, 0)

    def to_core(z_hi_of):
        shard = z_hi_of * 2 + 1 - core
        return remote(term.at[shard], pair_got.at[z_hi_of], t_sent.at[z_hi_of], t_got.at[z_hi_of], core_peer)

    loads[4].wait()
    gradient(far_dp + 1 - 2 * core)
    to_core(1 - z_hi).start()
    gradient(far_dp)
    to_core(1 - z_hi).wait_recv()
    z_send[...] = (term[far_dp].astype(F32) + pair_got[1 - z_hi].astype(F32)).astype(BF16)
    z_copy = remote(z_send, z_got, t_sent.at[2], t_got.at[2], far_peer)
    z_copy.start()
    gradient(near_dp)
    to_core(z_hi).start()
    gradient(dp)
    to_core(z_hi).wait_recv()
    z_copy.wait_recv()
    grad_total = pre
    grad_total[pl.ds(0, shard_rows), :] = term[dp].astype(F32) + pair_got[z_hi].astype(F32) + z_got[...].astype(F32)
    grad_small[0] = grad_total[pl.ds(0, shard_rows), :].astype(BF16)

    swap_grad.start()
    swap_grad.second()
    swap_grad.along_z()
    swap_grad.fourth()
    swap_grad.last()
    swap_state.wait_last()
    swap_grad.wait_last()

    swap_state.wait_first()
    w_far.wait_send()
    w_near.wait_send()
    moved = (pair[0] == me) | (pair[1] == me)

    def update(i, _):
        rows = pl.ds(pl.multiple_of(i * 64, 16), 64)
        total = jnp.where(moved, swap_grad.got[0, rows, :].astype(F32), grad_total[rows, :])
        old = [
            jnp.where(moved, swap_state.got[c, rows, :].astype(F32), state[c, rows, :].astype(F32))
            for c in range(3)
        ]
        moment_one = beta_one * old[1] + (1.0 - beta_one) * total
        moment_two = beta_two * old[2] + (1.0 - beta_two) * total * total
        state[0, rows, :] = (old[0] - step_size * moment_one / (jnp.sqrt(moment_two) + epsilon)).astype(BF16)
        state[1, rows, :] = moment_one.astype(BF16)
        state[2, rows, :] = moment_two.astype(BF16)
        return 0

    lax.fori_loop(0, shard_rows // 64, update, 0)
    stores = [
        pltpu.make_async_copy(state.at[c], out, local_sem.at[5 + c]) for c, out in enumerate((w_out, m_out, v_out))
    ]
    for store in stores:
        store.start()

    for copy in hops + passed_hop + tuple(g_lines):
        copy.wait_send()
    for route in (route_g, route_mine, route_other):
        route.wait_sent()
    w_pass.wait_send()
    to_core(0).wait_send()
    to_core(1).wait_send()
    z_copy.wait_send()
    swap_state.wait_sent()
    swap_grad.wait_first()
    swap_grad.wait_sent()
    for store in stores:
        store.wait()


def expert_update(tokens, routes, grads, owner, moves, w_shard, m_shard, v_shard, residual):
    tok_rows, feats = tokens.shape
    hidden = grads.shape[1]
    count = owner.shape[0]
    shard_rows = w_shard.shape[0]
    rows = count * CAP
    dma = pltpu.SemaphoreType.DMA
    vmem = pl.BlockSpec(memory_space=pltpu.VMEM)
    hbm = pl.BlockSpec(memory_space=pl.ANY)
    return pl.pallas_call(
        kernel,
        out_shape=[jax.ShapeDtypeStruct((shard_rows, hidden), BF16)] * 3,
        in_specs=[
            pl.BlockSpec(memory_space=pltpu.SMEM), vmem, vmem, hbm, hbm, hbm, hbm, hbm, hbm
        ],
        out_specs=[hbm] * 3,
        scratch_shapes=[
            pltpu.VMEM((NZ, TOP, tok_rows), jnp.int32),
            pltpu.VMEM((NZ, tok_rows, feats), BF16),
            pltpu.VMEM((2, NY, NX, 2 * CAP, feats), BF16),
            pltpu.VMEM((2, 2, 4, 4, 2 * CAP, feats // 2), BF16),
            pltpu.VMEM((rows, feats), BF16),
            pltpu.VMEM((NY, NX, NZ, CAP, hidden), BF16),
            pltpu.VMEM((2, 4, 4, 2, CAP, hidden), BF16),
            pltpu.VMEM((NY, NX, NZ, CAP, hidden), BF16),
            pltpu.VMEM((NZ, NY, NX, CAP, hidden), BF16),
            pltpu.VMEM((feats, hidden), BF16),
            pltpu.VMEM((max(rows // 4, shard_rows), hidden), F32),
            pltpu.VMEM((rows, hidden), BF16),
            pltpu.VMEM((4, shard_rows, hidden), BF16),
            pltpu.VMEM((2, shard_rows, hidden), BF16),
            pltpu.VMEM((shard_rows, hidden), BF16),
            pltpu.VMEM((shard_rows, hidden), BF16),
            dma((10,)),
            dma((3,)), dma((NZ,)), dma((3,)), dma((NZ,)),
            dma((NZ,)), dma((NZ,)),
            dma((3,)), dma((3,)), dma((3,)), dma((3,)),
            pltpu.VMEM((3, shard_rows, hidden), BF16),
            pltpu.VMEM((1, shard_rows, hidden), BF16),
            *route_sems(), *route_sems(), *route_sems(),
            *swap_scratch(3, shard_rows, hidden),
            *swap_scratch(1, shard_rows, hidden),
        ],
        compiler_params=pltpu.CompilerParams(
            collective_id=0, has_side_effects=True, vmem_limit_bytes=62 * 2**20
        ),
        name="expert_update",
    )(
        moves, routes.T, owner[None, :], tokens, grads, w_shard, m_shard, v_shard,
        residual.reshape(-1, shard_rows, hidden),
    )


def shards(tokens, routes, grad_act, owner, moves, weight, first_moment, second_moment, residual):
    hidden = grad_act.shape[2]
    new_w, new_m, new_v = expert_update(
        tokens, routes, grad_act.reshape(-1, hidden), owner, moves, weight[0], first_moment[0], second_moment[0],
        residual[0, 0],
    )
    return (new_w[None], new_m[None], new_v[None])


def solution(mesh):
    return jax.shard_map(
        shards,
        mesh=mesh,
        in_specs=(
            P(("dp", "expert"), None),
            P(("dp", "expert"), None),
            P(("dp", "expert"), None, None),
            P(),
            P(),
            P("expert", "dp", None),
            P("expert", "dp", None),
            P("expert", "dp", None),
            P("dp", "expert", None, None),
        ),
        out_specs=(P("expert", "dp", None), P("expert", "dp", None), P("expert", "dp", None)),
        check_vma=False,
    )
```

```python
import functools

import jax
import jax.numpy as jnp
from jax import lax
from jax.experimental import pallas as pl
from jax.experimental.pallas import tpu as pltpu
from jax.sharding import PartitionSpec as P

MESH = pl.DeviceIdType.MESH
F32 = jnp.float32
BF16 = jnp.bfloat16

beta_one = 0.9
beta_two = 0.95
step_size = 0.05
epsilon = 1e-08

NY, NX, NZ = 4, 4, 4
PLANE = NY * NX
CAP = 24
TOP = 8


def silu_slope(values):
    sigma = jax.nn.sigmoid(values)
    return sigma * (1.0 + values * (1.0 - sigma))


class Swap:
    def __init__(self, src, pair, spot, at, remote, scratch):
        (self.got1, self.out2, self.got2, self.out3, self.got3, self.out4, self.got4, self.back, self.got,
         self.sent, self.come) = scratch
        self.src, self.pair, self.at, self.remote = src, pair, at, remote
        self.y, self.x, self.z = spot
        self.ys = [p // (NX * NZ) for p in pair]
        self.xs = [(p // NZ) % NX for p in pair]
        self.zs = [p % NZ for p in pair]
        self.half = src.shape[1] // 2
        self.piece = self.half // 4
        self.small = self.piece // 4

    def axes(self, half):
        along = [(self.x, self.xs), (self.y, self.ys)]
        return along if half == 0 else along[::-1]

    def peer(self, half, first, d):
        if first == (half == 0):
            to = lax.rem(self.x + d, NX)
            return to, self.at(self.y * NX + to, self.z), self.x
        to = lax.rem(self.y + d, NY)
        return to, self.at(to * NX + self.x, self.z), self.y

    def rows1(self, half, to):
        return pl.ds(pl.multiple_of(half * self.half + to * self.piece, 16), self.piece)

    def rows2(self, to):
        return pl.ds(pl.multiple_of(to * self.small, 16), self.small)

    def copy1(self, half, d, arriving=False):
        to, device, mine = self.peer(half, True, d)
        return self.remote(self.src.at[:, self.rows1(half, to)], self.got1.at[half, to if arriving else mine],
                           self.sent.at[0, half, to], self.come.at[0, half, to if arriving else mine], device)

    def copy2(self, half, d, arriving=False):
        to, device, mine = self.peer(half, False, d)
        return self.remote(self.out2.at[half, :, self.rows2(to)], self.got2.at[half, to if arriving else mine],
                           self.sent.at[1, half, to], self.come.at[1, half, to if arriving else mine], device)

    def copy3(self, half, d, arriving=False):
        to = lax.rem(self.z + d, NZ)
        device = self.at(self.y * NX + self.x, to)
        mine = to if arriving else self.z
        return self.remote(self.out3.at[half], self.got3.at[half, mine],
                           self.sent.at[2, half, to], self.come.at[2, half, mine], device)

    def copy4(self, half, d, arriving=False):
        to, device, mine = self.peer(half, False, d)
        return self.remote(self.out4.at[half, to], self.got4.at[half, to if arriving else mine],
                           self.sent.at[3, half, to], self.come.at[3, half, to if arriving else mine], device)

    def copy5(self, half, d, arriving=False):
        to, device, mine = self.peer(half, True, d)
        return self.remote(self.back.at[half, to], self.got.at[:, self.rows1(half, to if arriving else mine)],
                           self.sent.at[4, half, to], self.come.at[4, half, to if arriving else mine], device)

    def each(self, act):
        for d in (1, 3, 2):
            for half in range(2):
                act(half, d)

    def start(self):
        self.each(lambda half, d: self.copy1(half, d).start())
        for half in range(2):
            mine = self.peer(half, True, 0)[0]
            self.got1[half, mine] = self.src[:, self.rows1(half, mine), :]

    def second(self):
        self.each(lambda half, d: self.copy1(half, d, True).wait_recv())
        for half in range(2):
            (_, firsts), (second, seconds) = self.axes(half)
            held = (second == seconds[0]) & (self.z == self.zs[0])
            self.out2[half] = self.got1[half, jnp.where(held, firsts[0], firsts[1])]
        self.each(lambda half, d: self.copy2(half, d).start())
        for half in range(2):
            mine = self.peer(half, False, 0)[0]
            self.got2[half, mine] = self.out2[half, :, self.rows2(mine), :]

    def along_z(self):
        self.each(lambda half, d: self.copy2(half, d, True).wait_recv())
        for half in range(2):
            seconds = self.axes(half)[1][1]
            self.out3[half] = self.got2[half, jnp.where(self.z == self.zs[0], seconds[0], seconds[1])]
        self.each(lambda half, d: self.copy3(half, d).start())
        for half in range(2):
            self.got3[half, self.z] = self.out3[half]

    def fourth(self):
        self.each(lambda half, d: self.copy3(half, d, True).wait_recv())
        plane = self.zs[0] == self.zs[1]
        for d in (1, 3, 2, 0):
            for half in range(2):
                seconds = self.axes(half)[1][1]
                to = self.peer(half, False, d)[0]
                takes = (to == seconds[1]) & (self.z == self.zs[1])
                kept = jnp.where(
                    plane,
                    self.got2[half, jnp.where(takes, seconds[0], seconds[1])],
                    self.got3[half, jnp.where(takes, self.zs[0], self.zs[1])],
                )
                if d:
                    self.out4[half, to] = kept
                    self.copy4(half, d).start()
                else:
                    self.got4[half, to] = kept

    def last(self):
        self.each(lambda half, d: self.copy4(half, d, True).wait_recv())
        for d in (1, 3, 2, 0):
            for half in range(2):
                (_, firsts), (_, seconds) = self.axes(half)
                row = (seconds[0] == seconds[1]) & (self.zs[0] == self.zs[1])
                to, device, _ = self.peer(half, True, d)
                index = jnp.where(self.pair[1] == device[1], firsts[0], firsts[1])
                for i in range(4):
                    rows = pl.ds(i * self.small, self.small)
                    part = jnp.where(row, self.got1[half, index, :, rows, :], self.got4[half, i])
                    if d:
                        self.back[half, to, :, rows, :] = part
                    else:
                        first = pl.multiple_of(half * self.half + to * self.piece + i * self.small, 16)
                        self.got[:, pl.ds(first, self.small), :] = part
                if d:
                    self.copy5(half, d).start()

    def wait_last(self):
        self.each(lambda half, d: self.copy5(half, d, True).wait_recv())

    def wait_first(self):
        self.each(lambda half, d: self.copy1(half, d).wait_send())

    def wait_sent(self):
        for copy in (self.copy2, self.copy3, self.copy4, self.copy5):
            self.each(lambda half, d: copy(half, d).wait_send())


class Route:
    def __init__(self, spot, at, remote, send, relay, own, passed, dest, sems):
        self.y, self.x, self.z = spot
        self.at, self.remote = at, remote
        self.send, self.relay, self.own, self.passed, self.dest = send, relay, own, passed, dest
        self.sent1, self.got1, self.sent2, self.got2, self.local = sems

    def spots(self, half):
        return (self.x, self.y) if half == 0 else (self.y, self.x)

    def device(self, half, first, to):
        along_x = first == (half == 0)
        return self.at(self.y * NX + to if along_x else to * NX + self.x, self.z)

    def hop1(self, half, d, arriving=False):
        mine = self.spots(half)[0]
        to = lax.rem(mine + d, 4)
        index = to if arriving else mine
        return self.remote(self.send(half, to), self.relay(half, index), self.sent1.at[half, to],
                           self.got1.at[half, index], self.device(half, True, to))

    def hop2(self, half, d, e, arriving=False):
        first, second = self.spots(half)
        come = lax.rem(first + d, 4)
        to = lax.rem(second + e, 4)
        piece = self.passed(half, come, to) if d else self.own(half, to)
        if not e:
            return pltpu.make_async_copy(piece, self.dest(half, come, second), self.local.at[half, come])
        index = to if arriving else second
        return self.remote(piece, self.dest(half, come, index), self.sent2.at[half, come, to],
                           self.got2.at[half, come, index], self.device(half, False, to))

    def start(self):
        for d in (1, 3, 2):
            for half in range(2):
                self.hop1(half, d).start()
        self.pass_on(0)

    def pass_on(self, d):
        for half in range(2):
            if d:
                self.hop1(half, d, True).wait_recv()
            for e in (1, 3, 2, 0):
                self.hop2(half, d, e).start()

    def relay_all(self):
        for d in (1, 3, 2):
            self.pass_on(d)

    def wait_all(self):
        for half in range(2):
            for d in range(4):
                for e in range(1, 4):
                    self.hop2(half, d, e, True).wait_recv()
                self.hop2(half, d, 0).wait()

    def wait_sent(self):
        for half in range(2):
            for d in range(4):
                if d:
                    self.hop1(half, d).wait_send()
                for e in range(1, 4):
                    self.hop2(half, d, e).wait_send()


def route_sems():
    dma = pltpu.SemaphoreType.DMA
    return [dma((2, 4)), dma((2, 4)), dma((2, 4, 4)), dma((2, 4, 4)), dma((2, 4))]


def swap_scratch(parts, rows, hidden):
    piece, small = rows // 8, rows // 32
    return [
        pltpu.VMEM((2, 4, parts, piece, hidden), BF16),
        pltpu.VMEM((2, parts, piece, hidden), BF16),
        pltpu.VMEM((2, 4, parts, small, hidden), BF16),
        pltpu.VMEM((2, parts, small, hidden), BF16),
        pltpu.VMEM((2, 4, parts, small, hidden), BF16),
        pltpu.VMEM((2, 4, parts, small, hidden), BF16),
        pltpu.VMEM((2, 4, parts, small, hidden), BF16),
        pltpu.VMEM((2, 4, parts, piece, hidden), BF16),
        pltpu.VMEM((parts, rows, hidden), BF16),
        pltpu.SemaphoreType.DMA((5, 2, 4)),
        pltpu.SemaphoreType.DMA((5, 2, 4)),
    ]


def kernel(
    moves, routes_t, owner_row, tokens, grads, w_shard, m_shard, v_shard, residual,
    w_out, m_out, v_out,
    codes, all_tokens, packed_x, relay_x, rows_x, packed_g, passed_g, relay_g, rows_g, w_full, pre, slopes,
    term, pair_got, z_send, z_got,
    local_sem, tok_sent, tok_got, code_sent, code_got,
    gz_sent, gz_got, w_sent, w_got, t_sent, t_got,
    state, grad_small, *rest,
):
    count = owner_row.shape[1]
    tok_rows, feats = tokens.shape
    hidden = grads.shape[1]
    pairs = grads.shape[0]
    shard_rows = w_shard.shape[0]
    scale = float(feats) ** -0.5

    dp = lax.axis_index("dp")
    me = lax.axis_index("expert")
    z_hi, core = dp // 2, dp % 2
    yx, z = me // NZ, me % NZ
    y, x = yx // NX, yx % NX

    def at(yx_to, z_to):
        return (dp, yx_to * NZ + z_to)

    turn = 1 - 2 * core

    def ring(step):
        p = lax.rem(z_hi * NZ + z + step + 2 * NZ, 2 * NZ)
        return ((p // NZ) * 2 + core, yx * NZ + p % NZ), p % NZ

    core_peer = (z_hi * 2 + 1 - core, me)
    far_peer = ((1 - z_hi) * 2 + core, me)

    def remote(src, dst, sent, got, to):
        return pltpu.make_async_remote_copy(
            src_ref=src, dst_ref=dst, send_sem=sent, recv_sem=got, device_id=to, device_id_type=MESH
        )

    held_grads = slopes.at[pl.ds(0, pairs)]
    loads = [
        pltpu.make_async_copy(tokens, all_tokens.at[z], local_sem.at[4]),
        pltpu.make_async_copy(w_shard, state.at[0], local_sem.at[5]),
        pltpu.make_async_copy(m_shard, state.at[1], local_sem.at[6]),
        pltpu.make_async_copy(v_shard, state.at[2], local_sem.at[7]),
        pltpu.make_async_copy(residual, term, local_sem.at[8]),
        pltpu.make_async_copy(grads, held_grads, local_sem.at[9]),
    ]
    for load in loads:
        load.start()

    barrier = pltpu.get_barrier_semaphore()
    for d in range(1, 4):
        pl.semaphore_signal(barrier, inc=1, device_id=at(y * NX + lax.rem(x + d, NX), z), device_id_type=MESH)
        pl.semaphore_signal(barrier, inc=1, device_id=at(lax.rem(y + d, NY) * NX + x, z), device_id_type=MESH)
    for dz in range(1, NZ):
        pl.semaphore_signal(barrier, inc=1, device_id=at(yx, lax.rem(z + dz, NZ)), device_id_type=MESH)
    for step in (1, -1, 2, -2):
        pl.semaphore_signal(barrier, inc=1, device_id=ring(step)[0], device_id_type=MESH)
    pl.semaphore_signal(barrier, inc=1, device_id=core_peer, device_id_type=MESH)
    pl.semaphore_signal(barrier, inc=1, device_id=far_peer, device_id_type=MESH)
    pl.semaphore_wait(barrier, 3 + 3 + NZ - 1 + 4 + 2)

    device_col = lax.broadcasted_iota(jnp.int32, (count, 1), 0)
    expert = lax.broadcasted_iota(jnp.int32, (count, count), 0) == lax.broadcasted_iota(jnp.int32, (count, count), 1)
    owner_col = jnp.sum(jnp.where(expert, owner_row[...], 0), axis=1, keepdims=True)
    before = (
        lax.broadcasted_iota(jnp.int32, (tok_rows, tok_rows), 0)
        < lax.broadcasted_iota(jnp.int32, (tok_rows, tok_rows), 1)
    ).astype(F32).astype(BF16)
    row_targets = [
        jnp.sum(jnp.where(device_col == routes_t[k : k + 1, :], owner_col, 0), axis=0, keepdims=True)
        for k in range(TOP)
    ]
    hits = [jnp.where(device_col == target, 1.0, 0.0) for target in row_targets]
    ranks = jnp.dot(sum(hits).astype(BF16), before, preferred_element_type=F32)
    target = jnp.concatenate(row_targets, axis=0)
    rank = jnp.concatenate([jnp.sum(hit * ranks, axis=0, keepdims=True) for hit in hits], axis=0)
    codes[z] = target * CAP + rank.astype(jnp.int32)
    loads[0].wait()

    def hop(source, step, sent):
        to = ring(step)[0]
        return (
            remote(all_tokens.at[source], all_tokens.at[source], tok_sent.at[sent], tok_got.at[source], to),
            remote(codes.at[source], codes.at[source], code_sent.at[sent], code_got.at[source], to),
        )

    behind = ring(-turn)[1]
    hops = hop(z, turn, 0) + hop(z, -turn, 1)
    passed_hop = hop(behind, turn, 2)

    def wait_hop(source):
        for copy in hop(source, 1, 0):
            copy.wait_recv()

    for copy in hops:
        copy.start()

    for load in loads[1:4]:
        load.wait()
    pair = (moves[1, 1], moves[0, 1])
    swaps = rest[3 * len(route_sems()) :]
    half_swap = len(swaps) // 2
    swap_state = Swap(state, pair, (y, x, z), at, remote, swaps[:half_swap])
    swap_grad = Swap(grad_small, pair, (y, x, z), at, remote, swaps[half_swap:])

    swap_state.start()

    spread = (
        lax.broadcasted_iota(jnp.int32, (tok_rows, pairs), 0)
        == lax.broadcasted_iota(jnp.int32, (tok_rows, pairs), 1) // TOP
    ).astype(F32).astype(BF16)
    slot_of = lax.broadcasted_iota(jnp.int32, (TOP, pairs), 0) == lax.broadcasted_iota(jnp.int32, (TOP, pairs), 1) % TOP
    flat_target, flat_rank = [
        jnp.sum(
            jnp.where(slot_of, jnp.dot(v.astype(BF16), spread, preferred_element_type=F32), 0.0), axis=0, keepdims=True
        )
        for v in (target.astype(F32), rank)
    ]
    flat_codes = (flat_target * CAP + flat_rank).astype(jnp.int32)

    group = NX * NZ * CAP

    spot = (y, x, z)
    n_sems = len(route_sems())
    route_g = Route(
        spot, at, remote,
        lambda half, to: packed_g.at[to, :, pl.ds(2, 2)] if half else packed_g.at[:, to, pl.ds(0, 2)],
        lambda half, come: passed_g.at[half, come],
        lambda half, to: packed_g.at[y, to, pl.ds(2, 2)] if half else packed_g.at[to, x, pl.ds(0, 2)],
        lambda half, come, to: passed_g.at[half, come, to],
        lambda half, first, second: (
            relay_g.at[first, second, pl.ds(2, 2)] if half else relay_g.at[second, first, pl.ds(0, 2)]
        ),
        rest[:n_sems],
    )
    loads[5].wait()
    for y_to in range(NY):
        slot = lax.broadcasted_iota(jnp.int32, (group, pairs), 0) + y_to * group
        pick = jnp.where(slot == flat_codes, 1.0, 0.0).astype(BF16)
        got = jnp.dot(pick, held_grads[...], preferred_element_type=F32)
        for x_to in range(NX):
            for z_to in range(NZ):
                first = (x_to * NZ + z_to) * CAP
                packed_g[y_to, x_to, z_to] = got[first : first + CAP].astype(BF16)
    route_g.start()

    block = 2 * CAP

    wide = feats // 2

    def pair_route(pair, sems):
        def cols(half):
            return pl.ds(half * wide, wide)

        def rows_of(half, first, second):
            src = first * NX + second if half else second * NX + first
            return rows_x.at[pl.ds(pl.multiple_of((pair * PLANE + src) * block, 16), block), cols(half)]

        return Route(
            spot, at, remote,
            lambda half, to: (
                packed_x.at[pair, to, :, :, cols(half)] if half else packed_x.at[pair, :, to, :, cols(half)]
            ),
            lambda half, come: relay_x.at[pair, half, come],
            lambda half, to: (
                packed_x.at[pair, y, to, :, cols(half)] if half else packed_x.at[pair, to, x, :, cols(half)]
            ),
            lambda half, come, to: relay_x.at[pair, half, come, to],
            rows_of,
            sems,
        )

    def pack_pair(pair, route):
        part = NX * block
        s = lax.broadcasted_iota(jnp.int32, (part, tok_rows), 0)
        to = (s * 1366) >> 16
        half = (s * 2731) >> 16
        rank = s - half * CAP
        for y_to in range(NY):
            want = ((y_to * NX + to) * NZ + z) * CAP + rank
            picks = []
            for sub in range(2):
                source = codes[pair * 2 + sub]
                mine = jnp.where(half == 2 * to + sub, want, -1)
                hit = mine == source[0:1, :]
                for k in range(1, TOP):
                    hit = hit | (mine == source[k : k + 1, :])
                picks.append(jnp.where(hit, 1.0, 0.0).astype(BF16))
            pick = jnp.concatenate(picks, axis=1)
            for c in range(2):
                both = all_tokens[pl.ds(pair * 2, 2), :, pl.ds(c * wide, wide)].reshape(2 * tok_rows, wide)
                got = jnp.dot(pick, both, preferred_element_type=F32).astype(BF16)
                packed_x[pair, y_to, :, :, pl.ds(c * wide, wide)] = got.reshape(NX, block, wide)
        route.start()

    my_pair = z // 2
    route_mine = pair_route(my_pair, rest[n_sems : 2 * n_sems])
    route_other = pair_route(1 - my_pair, rest[2 * n_sems : 3 * n_sems])
    wait_hop(behind)
    for copy in passed_hop:
        copy.start()
    wait_hop(ring(turn)[1])
    pack_pair(my_pair, route_mine)
    swap_state.second()

    def w_rows(owner_dp):
        return w_full.at[pl.ds(pl.multiple_of(owner_dp * shard_rows, 16), shard_rows)]

    w_full[pl.ds(pl.multiple_of(dp * shard_rows, 16), shard_rows), :] = state[0]
    far_dp = (1 - z_hi) * 2 + core
    near_dp = z_hi * 2 + 1 - core
    w_far = remote(state.at[0], w_rows(dp), w_sent.at[0], w_got.at[0], far_peer)
    w_near = remote(state.at[0], w_rows(dp), w_sent.at[1], w_got.at[1], core_peer)
    w_pass = remote(w_rows(far_dp), w_rows(far_dp), w_sent.at[2], w_got.at[2], core_peer)
    w_far.start()
    w_near.start()

    route_g.relay_all()
    wait_hop(ring(2 * turn)[1])
    pack_pair(1 - my_pair, route_other)
    swap_state.along_z()
    route_mine.relay_all()

    route_g.wait_all()

    def g_line(step):
        device, z_to = ring(step)
        return remote(relay_g.at[:, :, z_to], rows_g.at[z], gz_sent.at[z_to], gz_got.at[z], device)

    g_lines = [g_line(2 * turn), g_line(turn), g_line(-turn)]
    for copy in g_lines:
        copy.start()
    self_rows = pltpu.make_async_copy(relay_g.at[:, :, z], rows_g.at[z], local_sem.at[3])
    self_rows.start()
    route_other.relay_all()
    swap_state.fourth()

    w_far.wait_recv()
    w_pass.start()
    w_near.wait_recv()
    w_pass.wait_recv()

    def wait_line(z_from):
        remote(
            relay_g.at[:, :, z_from], rows_g.at[z_from], gz_sent.at[z_from], gz_got.at[z_from], at(yx, z_from)
        ).wait_recv()

    def forward(pair):
        per = PLANE // 2
        for part in range(2):
            base = pl.multiple_of((pair * PLANE + part * per) * block, 16)
            pre[pl.ds(0, per * block), :] = jnp.dot(
                rows_x[pl.ds(base, per * block), :], w_full[...], preferred_element_type=F32
            ) * scale

            def body(i, _):
                rows = pl.ds(pl.multiple_of(i * block, 16), block)
                src_y, src_x = part * (per // NX) + i // NX, i % NX
                g = jnp.concatenate(
                    [rows_g[pair * 2, src_y, src_x].astype(F32), rows_g[pair * 2 + 1, src_y, src_x].astype(F32)], axis=0
                )
                slope = (g * silu_slope(pre[rows, :])).astype(BF16)
                slopes[pl.ds(pl.multiple_of(base + i * block, 16), block), :] = slope
                return 0

            lax.fori_loop(0, per, body, 0)

    route_mine.wait_all()
    self_rows.wait()
    wait_line(my_pair * 4 + 1 - z)
    forward(my_pair)
    route_other.wait_all()
    for sub in range(2):
        wait_line((1 - my_pair) * 2 + sub)
    forward(1 - my_pair)
    swap_state.last()

    tile = shard_rows // 2

    def gradient(shard):
        def body(i, _):
            first = pl.multiple_of(shard * shard_rows + i * tile, 128)
            part = lax.dot_general(
                rows_x[:, pl.ds(first, tile)], slopes[...], (((0,), (0,)), ((), ())),
                preferred_element_type=F32,
            )
            rows = pl.ds(pl.multiple_of(i * tile, 16), tile)
            term[shard, rows, :] = (part * scale + term[shard, rows, :].astype(F32)).astype(BF16)
            return 0

        lax.fori_loop(0, 2, body, 0)

    def to_core(z_hi_of):
        shard = z_hi_of * 2 + 1 - core
        return remote(term.at[shard], pair_got.at[z_hi_of], t_sent.at[z_hi_of], t_got.at[z_hi_of], core_peer)

    loads[4].wait()
    gradient(far_dp + 1 - 2 * core)
    to_core(1 - z_hi).start()
    gradient(far_dp)
    to_core(1 - z_hi).wait_recv()
    z_send[...] = (term[far_dp].astype(F32) + pair_got[1 - z_hi].astype(F32)).astype(BF16)
    z_copy = remote(z_send, z_got, t_sent.at[2], t_got.at[2], far_peer)
    z_copy.start()
    gradient(near_dp)
    to_core(z_hi).start()
    gradient(dp)
    to_core(z_hi).wait_recv()
    z_copy.wait_recv()
    grad_total = pre
    grad_total[pl.ds(0, shard_rows), :] = term[dp].astype(F32) + pair_got[z_hi].astype(F32) + z_got[...].astype(F32)
    grad_small[0] = grad_total[pl.ds(0, shard_rows), :].astype(BF16)

    swap_grad.start()
    swap_grad.second()
    swap_grad.along_z()
    swap_grad.fourth()
    swap_grad.last()
    swap_state.wait_last()
    swap_grad.wait_last()

    swap_state.wait_first()
    w_far.wait_send()
    w_near.wait_send()
    moved = (pair[0] == me) | (pair[1] == me)

    def update(i, _):
        rows = pl.ds(pl.multiple_of(i * 64, 16), 64)
        total = jnp.where(moved, swap_grad.got[0, rows, :].astype(F32), grad_total[rows, :])
        old = [
            jnp.where(moved, swap_state.got[c, rows, :].astype(F32), state[c, rows, :].astype(F32))
            for c in range(3)
        ]
        moment_one = beta_one * old[1] + (1.0 - beta_one) * total
        moment_two = beta_two * old[2] + (1.0 - beta_two) * total * total
        state[0, rows, :] = (old[0] - step_size * moment_one / (jnp.sqrt(moment_two) + epsilon)).astype(BF16)
        state[1, rows, :] = moment_one.astype(BF16)
        state[2, rows, :] = moment_two.astype(BF16)
        return 0

    lax.fori_loop(0, shard_rows // 64, update, 0)
    stores = [
        pltpu.make_async_copy(state.at[c], out, local_sem.at[5 + c]) for c, out in enumerate((w_out, m_out, v_out))
    ]
    for store in stores:
        store.start()

    for copy in hops + passed_hop + tuple(g_lines):
        copy.wait_send()
    for route in (route_g, route_mine, route_other):
        route.wait_sent()
    w_pass.wait_send()
    to_core(0).wait_send()
    to_core(1).wait_send()
    z_copy.wait_send()
    swap_state.wait_sent()
    swap_grad.wait_first()
    swap_grad.wait_sent()
    for store in stores:
        store.wait()


def expert_update(tokens, routes, grads, owner, moves, w_shard, m_shard, v_shard, residual):
    tok_rows, feats = tokens.shape
    hidden = grads.shape[1]
    count = owner.shape[0]
    shard_rows = w_shard.shape[0]
    rows = count * CAP
    dma = pltpu.SemaphoreType.DMA
    vmem = pl.BlockSpec(memory_space=pltpu.VMEM)
    hbm = pl.BlockSpec(memory_space=pl.ANY)
    return pl.pallas_call(
        kernel,
        out_shape=[jax.ShapeDtypeStruct((shard_rows, hidden), BF16)] * 3,
        in_specs=[
            pl.BlockSpec(memory_space=pltpu.SMEM), vmem, vmem, hbm, hbm, hbm, hbm, hbm, hbm
        ],
        out_specs=[hbm] * 3,
        scratch_shapes=[
            pltpu.VMEM((NZ, TOP, tok_rows), jnp.int32),
            pltpu.VMEM((NZ, tok_rows, feats), BF16),
            pltpu.VMEM((2, NY, NX, 2 * CAP, feats), BF16),
            pltpu.VMEM((2, 2, 4, 4, 2 * CAP, feats // 2), BF16),
            pltpu.VMEM((rows, feats), BF16),
            pltpu.VMEM((NY, NX, NZ, CAP, hidden), BF16),
            pltpu.VMEM((2, 4, 4, 2, CAP, hidden), BF16),
            pltpu.VMEM((NY, NX, NZ, CAP, hidden), BF16),
            pltpu.VMEM((NZ, NY, NX, CAP, hidden), BF16),
            pltpu.VMEM((feats, hidden), BF16),
            pltpu.VMEM((max(rows // 4, shard_rows), hidden), F32),
            pltpu.VMEM((rows, hidden), BF16),
            pltpu.VMEM((4, shard_rows, hidden), BF16),
            pltpu.VMEM((2, shard_rows, hidden), BF16),
            pltpu.VMEM((shard_rows, hidden), BF16),
            pltpu.VMEM((shard_rows, hidden), BF16),
            dma((10,)),
            dma((3,)), dma((NZ,)), dma((3,)), dma((NZ,)),
            dma((NZ,)), dma((NZ,)),
            dma((3,)), dma((3,)), dma((3,)), dma((3,)),
            pltpu.VMEM((3, shard_rows, hidden), BF16),
            pltpu.VMEM((1, shard_rows, hidden), BF16),
            *route_sems(), *route_sems(), *route_sems(),
            *swap_scratch(3, shard_rows, hidden),
            *swap_scratch(1, shard_rows, hidden),
        ],
        compiler_params=pltpu.CompilerParams(
            collective_id=0, has_side_effects=True, vmem_limit_bytes=62 * 2**20
        ),
        name="expert_update",
    )(
        moves, routes.T, owner[None, :], tokens, grads, w_shard, m_shard, v_shard,
        residual.reshape(-1, shard_rows, hidden),
    )


def hand_over(w_in, m_in, v_in, w_out, m_out, v_out):
    w_out[...] = w_in[...]
    m_out[...] = m_in[...]
    v_out[...] = v_in[...]


def shards(tokens, routes, grad_act, owner, moves, weight, first_moment, second_moment, residual):
    hidden = grad_act.shape[2]
    new_w, new_m, new_v = expert_update(
        tokens, routes, grad_act.reshape(-1, hidden), owner, moves, weight[0], first_moment[0], second_moment[0],
        residual[0, 0],
    )
    news = (new_w[None], new_m[None], new_v[None])
    part = pl.BlockSpec((1, new_w.shape[0] // 4, hidden), lambda i: (0, i, 0))
    return pl.pallas_call(
        hand_over,
        grid=(4,),
        out_shape=[jax.ShapeDtypeStruct(new.shape, new.dtype) for new in news],
        in_specs=[part] * 3,
        out_specs=[part] * 3,
        name="finish",
    )(*news)


def solution(mesh):
    return jax.shard_map(
        shards,
        mesh=mesh,
        in_specs=(
            P(("dp", "expert"), None),
            P(("dp", "expert"), None),
            P(("dp", "expert"), None, None),
            P(),
            P(),
            P("expert", "dp", None),
            P("expert", "dp", None),
            P("expert", "dp", None),
            P("dp", "expert", None, None),
        ),
        out_specs=(P("expert", "dp", None), P("expert", "dp", None), P("expert", "dp", None)),
        check_vma=False,
    )
```
